32 devices in a mesh: dp: 8 (over z, x), tensor: 4 (over y, core).
Axes of the slice: x: 2, y: 2, z: 4, core: 2. Of those that a mesh axis runs over, the one named last changes fastest.
Arguments:
- block_input: bfloat16 [16, 1024, 1024], P('dp'), may hold values from -6 to 6
- segment_ids: int32 [16, 1024], P('dp'), may hold values from 0 to 7, never falling along the last dimension, each value on 1 to 512 neighbouring positions
- pad_mask: int32 [16, 1024], P('dp'), may hold values from 0 to 1, as said below
- norm_gain: float32 [1024], replicated, may hold values from 0.1 to 1.9
- ema_forget: float32 [1024, 16], P('tensor'), may hold values from 0.001 to 0.05
- ema_mix: float32 [1024, 16], P('tensor'), may hold values from -4 to 4
- ema_skip: float32 [1024], P('tensor'), may hold values from -4 to 4
- proj_shared: bfloat16 [1024, 128], replicated, may hold values from -0.1875 to 0.1875
- query_gain: float32 [128], replicated, may hold values from -12 to 12
- query_bias: float32 [128], replicated, may hold values from -3 to 3
- key_gain: float32 [128], replicated, may hold values from -12 to 12
- proj_value: bfloat16 [1024, 2048], P(None, 'tensor'), may hold values from -0.1875 to 0.1875
- proj_reset: bfloat16 [1024, 2048], P(None, 'tensor'), may hold values from -0.1875 to 0.1875
- proj_out: bfloat16 [2048, 1024], P('tensor'), may hold values from -1 to 1
- ffn_gain: float32 [1024], replicated, may hold values from 0.1 to 1.9
- ffn_up: bfloat16 [1024, 4096], P(None, 'tensor'), may hold values from -0.1875 to 0.1875
- ffn_down: bfloat16 [4096, 1024], P('tensor'), may hold values from -0.09375 to 0.09375
- cotangent: bfloat16 [16, 1024, 1024], P('dp', 'tensor'), may hold values from -6 to 6
Outputs:
- block_output: bfloat16 [16, 1024, 1024], P('dp', 'tensor')
- grad_input: bfloat16 [16, 1024, 1024], P('dp', 'tensor')
- grad_norm_gain: float32 [1024], replicated
- grad_forget: float32 [1024, 16], P(('tensor', 'dp'))
- grad_mix: float32 [1024, 16], P(('tensor', 'dp'))
- grad_skip: float32 [1024], P(('tensor', 'dp'))
- grad_shared: float32 [1024, 128], P(('tensor', 'dp'))
- grad_query_gain: float32 [128], replicated
- grad_query_bias: float32 [128], replicated
- grad_key_gain: float32 [128], replicated
- grad_value: float32 [1024, 2048], P('dp', 'tensor')
- grad_reset: float32 [1024, 2048], P('dp', 'tensor')
- grad_out: float32 [2048, 1024], P(('tensor', 'dp'))
- grad_ffn_gain: float32 [1024], replicated
- grad_ffn_up: float32 [1024, 4096], P('dp', 'tensor')
- grad_ffn_down: float32 [4096, 1024], P(('tensor', 'dp'))
The draws below stay inside these ranges and needn't reach their ends.
Inputs may be any that keep to these rules, and one draw needn't show every extreme that they name: `segment_ids`: within each row the document numbers never fall; each of the 8 documents has 1 to 512 tokens. `pad_mask`: each row is ones followed by zeros.
All inputs are finite; a program needn't handle non-finite values.
Results may differ from the reference program's by a relative error of at most 0.025.
Values may be sent and summed in bfloat16 or wider, within the bound.
No kernel may reach another device: no remote copies, remote signals or barrier semaphores. Data moves between devices by JAX's collectives and lax.ppermute only.
A program may use at most 512 MiB of HBM per device.

```python
import math
import jax
import jax.numpy as jnp
import numpy as np
from jax import lax

D = 1024
Z = 128
VDIM = 2048
H = 16
FF = 4096
BLOCK = 1024
LEN = 1024
DOCS = 8
SEQS = 16
N_TENSOR = 4


def draw_pad_mask(key, part):
    tails = jax.random.randint(key, (SEQS, 1), 0, LEN // 8 + 1)
    places = jnp.arange(LEN, dtype=jnp.int32)[None, :]
    return (places < LEN - tails).astype(jnp.int32)


def level_of(stream_key, extent, cuts, low, high):
    def one(dim, parts):
        steps = jax.random.uniform(jax.random.fold_in(jax.random.fold_in(stream_key, 6), dim), (parts,), jnp.float32, low / len(cuts), high / len(cuts))
        return jnp.repeat(jnp.exp(steps), extent[dim] // parts).reshape((-1,) + (1,) * (len(extent) - dim - 1))

    level = one(*cuts[0])
    for cut in cuts[1:]:
        level = level * one(*cut)
    return level


def split_up(amount, total, reach, lean):
    portions = [(1 << 20) // math.isqrt(grade ** lean) + 1 for grade in range(2, amount + 1)]
    surplus, holding = total - reach - (amount - 1), [1] * (amount - 1)
    while surplus > 0:
        movable = [i for i in range(amount - 1) if holding[i] < reach]
        pool, remaining = sum([portions[i] for i in movable]), surplus
        for i in movable:
            more = min(reach - holding[i], max(1, remaining * portions[i] // pool), surplus)
            holding[i] = holding[i] + more
            surplus = surplus - more
    return np.array([reach] + holding)


def uneven_parts(stream_key, number_of, total, bound, skew):
    if number_of == 2:
        one = jax.random.randint(stream_key, (), max(1, total - bound), min(bound, total - 1) + 1)
        return jnp.stack([one, total - one])
    sizes = jnp.asarray(split_up(number_of, total, bound, skew), jnp.int32)
    twos = (number_of - 1) // 2
    donor, receiver = sizes[1:1 + 2 * twos:2], sizes[2:2 + 2 * twos:2]
    margin = jnp.minimum(donor - 1, bound - receiver)
    shifted = jax.random.randint(jax.random.fold_in(stream_key, 1), (twos,), 0, 1 << 20) % (margin + 1)
    sizes = sizes.at[1:1 + 2 * twos:2].set(donor - shifted).at[2:2 + 2 * twos:2].set(receiver + shifted)
    return sizes[jax.random.permutation(jax.random.fold_in(stream_key, 2), number_of)]


def noise(own_key, dims, deviation, bound, cuts=(), held_as=jnp.bfloat16):
    values = jax.random.normal(own_key, dims, jnp.float32) * deviation
    if len(cuts) > 0:
        values = level_of(own_key, dims, cuts, -0.22, 0.18) * values
    return jnp.clip(values, min=-bound, max=bound).astype(held_as)


def setup_inputs(seed: int = 0) -> dict:
    key_list = jax.random.split(jax.random.key(seed), 19)
    block_input = noise(key_list[0], (SEQS, LEN, D), 1.0, 6.0, ((0, 8),))
    segment_ids = jax.vmap(lambda own: jnp.searchsorted(jnp.cumsum(uneven_parts(own, DOCS, LEN, LEN // 2, 2)), jnp.arange(LEN), side="right"))(jax.random.split(key_list[1], SEQS)).reshape((SEQS, LEN)).astype(jnp.int32)
    pad_mask = draw_pad_mask(jax.random.fold_in(key_list[18], 71), 0)
    norm_gain = jnp.clip(1.0 + 0.18 * jax.random.normal(key_list[3], (D,), jnp.float32), 0.1, 1.9)
    ema_forget = jnp.clip(jnp.exp(math.log(0.05) - 3.912023 * jax.random.uniform(key_list[4], (D, H), jnp.float32) ** level_of(key_list[4], (D, H), ((0, 4),), -0.2, 0.2)), 0.001, 0.05)
    ema_mix = noise(key_list[5], (D, H), 1.0, 4.0, ((0, 4),), jnp.float32)
    ema_skip = noise(key_list[6], (D,), 1.0, 4.0, ((0, 4),), jnp.float32)
    proj_shared = noise(key_list[7], (D, Z), D ** -0.5, 0.1875)
    query_gain = noise(key_list[8], (Z,), 3.0, 12.0, (), jnp.float32)
    query_bias = noise(key_list[9], (Z,), 0.5, 3.0, (), jnp.float32)
    key_gain = noise(key_list[10], (Z,), 3.0, 12.0, (), jnp.float32)
    proj_value = noise(key_list[11], (D, VDIM), D ** -0.5, 0.1875, ((1, 4),))
    proj_reset = noise(key_list[12], (D, VDIM), D ** -0.5, 0.1875, ((1, 4),))
    proj_out = noise(key_list[13], (VDIM, D), (VDIM // 64) ** -0.5, 1.0, ((0, 4),))
    ffn_gain = jnp.clip(1.0 + 0.18 * jax.random.normal(key_list[14], (D,), jnp.float32), 0.1, 1.9)
    ffn_up = noise(key_list[15], (D, FF), D ** -0.5, 0.1875, ((1, 4),))
    ffn_down = noise(key_list[16], (FF, D), FF ** -0.5, 0.09375, ((0, 4),))
    cotangent = noise(key_list[17], (SEQS, LEN, D), 1.0, 6.0, ((0, 8), (1, 4)))
    return dict(block_input=block_input, segment_ids=segment_ids, pad_mask=pad_mask, norm_gain=norm_gain, ema_forget=ema_forget, ema_mix=ema_mix, ema_skip=ema_skip, proj_shared=proj_shared, query_gain=query_gain, query_bias=query_bias, key_gain=key_gain, proj_value=proj_value, proj_reset=proj_reset, proj_out=proj_out, ffn_gain=ffn_gain, ffn_up=ffn_up, ffn_down=ffn_down, cotangent=cotangent)


epsilon = 1e-06
precise = lax.Precision.HIGHEST

@jax.custom_vjp
def low(v):
    return lax.optimization_barrier(v.astype(jnp.bfloat16)).astype(jnp.float32)

@jax.custom_vjp
def low_back(v):
    return v

def low_keep(v):
    return (low(v), None)

def low_pass(kept, grad):
    return (grad,)

def back_keep(v):
    return (v, None)

def back_low(kept, grad):
    return (low(grad),)
low.defvjp(low_keep, low_pass)
low_back.defvjp(back_keep, back_low)

def matmul_hi(left, right):
    return jnp.dot(left, right, precision=precise)

def rms_norm(values, gain):
    return values * lax.rsqrt(lax.optimization_barrier(jnp.mean(values * values, axis=-1, keepdims=True)) + epsilon) * gain

def moving_average(source, starts, forget, mix, skip):

    def advance(state, pieces):
        value, start_flag = pieces
        state = (1.0 - forget) * (1.0 - start_flag) * state + forget * value[:, None]
        return (state, lax.optimization_barrier(jnp.sum(mix * state, axis=1)))
    _, mixed = lax.scan(jax.checkpoint(advance), jnp.zeros(forget.shape, forget.dtype), (source, starts))
    return mixed + skip * source

def attend(query, key, values, segments, padding):
    group_cols = VDIM // N_TENSOR
    score_scale = 1.0 / math.sqrt(Z)
    places = jnp.arange(BLOCK, dtype=jnp.int32)

    def one_block(pieces):
        query_c, key_c, values_c, seg_c, pad_c = pieces
        scores = matmul_hi(query_c, key_c.T) * score_scale
        allowed = (seg_c[:, None] == seg_c[None, :]) & ((pad_c[None, :] > 0) | (places[:, None] == places[None, :]))
        outputs = []
        for group in range(N_TENSOR):
            masked = jnp.where(allowed, low_back(scores), -1000000000.0)
            prob = low(jax.nn.softmax(masked, axis=-1))
            outputs.append(matmul_hi(prob, values_c[:, group * group_cols:(group + 1) * group_cols]))
        return jnp.concatenate(outputs, axis=1)
    length = query.shape[0]
    blocks = length // BLOCK
    result = lax.map(jax.checkpoint(one_block), (query.reshape(blocks, BLOCK, -1), key.reshape(blocks, BLOCK, -1), values.reshape(blocks, BLOCK, -1), segments.reshape(blocks, BLOCK), padding.reshape(blocks, BLOCK)))
    return result.reshape(length, -1)

def layer(inputs, params, segments, padding):
    norm_gain, ema_forget, ema_mix, ema_skip, proj_shared, query_gain, query_bias, key_gain, proj_value, proj_reset, proj_out, ffn_gain, ffn_up, ffn_down = params
    starts = jnp.concatenate([jnp.ones((1,), inputs.dtype), (segments[1:] != segments[:-1]).astype(inputs.dtype)])
    pad_float = padding.astype(inputs.dtype)
    normed = low(rms_norm(inputs, norm_gain))
    mixed = moving_average(normed * pad_float[:, None], starts, ema_forget, ema_mix, ema_skip)
    ema_out = low(jax.nn.silu(mixed))
    shared = jax.nn.silu(low_back(matmul_hi(ema_out, proj_shared)))
    query = low(shared * query_gain + query_bias)
    key = low(shared * key_gain)
    values = low(jax.nn.silu(low_back(matmul_hi(normed, proj_value))))
    reset = jax.nn.silu(low_back(matmul_hi(ema_out, proj_reset)))
    attn = low_back(attend(query, key, values, segments, padding))
    heard = low(attn * reset)
    middle = inputs + low_back(matmul_hi(heard, proj_out))
    normed_two = low(rms_norm(middle, ffn_gain))
    hidden = low(jax.nn.silu(low_back(matmul_hi(normed_two, ffn_up))))
    return middle + matmul_hi(hidden, ffn_down)

def add_pair(first_item, second_item):
    return first_item + second_item

def reference(block_input, segment_ids, pad_mask, norm_gain, ema_forget, ema_mix, ema_skip, proj_shared, query_gain, query_bias, key_gain, proj_value, proj_reset, proj_out, ffn_gain, ffn_up, ffn_down, cotangent):
    params = tuple((param.astype(jnp.float32) for param in (norm_gain, ema_forget, ema_mix, ema_skip, proj_shared, query_gain, query_bias, key_gain, proj_value, proj_reset, proj_out, ffn_gain, ffn_up, ffn_down)))
    zero_grads = jax.tree.map(jnp.zeros_like, params)

    def one_sequence(totals, pieces):
        inputs, segments, padding, grad_out = pieces

        def forward(values, weights):
            return layer(values, weights, segments, padding)
        result, pull = jax.vjp(forward, inputs.astype(jnp.float32), params)
        grad_in, grad_params = pull(grad_out.astype(jnp.float32))
        totals = jax.tree.map(add_pair, totals, grad_params)
        return (totals, (result.astype(jnp.bfloat16), grad_in.astype(jnp.bfloat16)))
    totals, (outputs, grad_inputs) = lax.scan(one_sequence, zero_grads, (block_input, segment_ids, pad_mask, cotangent))
    return (outputs, grad_inputs, totals[0], totals[1], totals[2], totals[3], totals[4], totals[5], totals[6], totals[7], totals[8], totals[9], totals[10], totals[11], totals[12], totals[13])
```

```python
import functools

import jax
import jax.numpy as jnp
from jax import lax
from jax.experimental import pallas as pl
from jax.experimental.pallas import tpu as pltpu
from jax.sharding import PartitionSpec as P

epsilon = 1e-06
dims_rows = (((0,), (0,)), ((), ()))
dims_cols = (((1,), (1,)), ((), ()))
f32 = jnp.float32
bf16 = jnp.bfloat16

CHUNK = 64
UNROLL = 8


def rms_norm(values, gain):
    return values * lax.rsqrt(jnp.mean(values * values, axis=-1, keepdims=True) + epsilon) * gain


def silu(values):
    return values * jax.nn.sigmoid(values)


def silu_slope(values):
    sigma = jax.nn.sigmoid(values)
    return sigma * (1.0 + values * (1.0 - sigma))


def matmul(left, right):
    return jnp.dot(left, right, preferred_element_type=f32)


def inner_rows(left, right):
    return lax.dot_general(left, right, dims_rows, preferred_element_type=f32)


def inner_cols(left, right):
    return lax.dot_general(left, right, dims_cols, preferred_element_type=f32)


def store_part(part_ref, row, values):
    for lane_group in range(part_ref.shape[0]):
        part_ref[lane_group, pl.ds(pl.multiple_of(row * 8, 8), 8), :] = values[
            :, lane_group * 128 : (lane_group + 1) * 128
        ]


def sum_parts(part_ref):
    columns = []
    for lane_group in range(part_ref.shape[0]):
        total = part_ref[lane_group, pl.ds(0, CHUNK, stride=8), :]
        for sub in range(1, 8):
            total = total + part_ref[lane_group, pl.ds(sub, CHUNK, stride=8), :]
        columns.append(total)
    return jnp.concatenate(columns, axis=1)


def ema_forward_kernel(alive_ref, x_ref, keep_ref, blend_ref, skip_ref, mixed_ref, out_ref, part_ref):
    states, width = keep_ref.shape
    length = x_ref.shape[0]
    keep = keep_ref[...]
    blend = blend_ref[...]
    half = states // 2

    def chunk(index, u):
        first = pl.multiple_of(index * CHUNK, CHUNK)

        def group(group_index, u):
            for step in range(UNROLL):
                row = group_index * UNROLL + step
                token = first + row
                u = (keep * alive_ref[token]) * u + x_ref[pl.ds(token, 1), :]
                term = u * blend
                store_part(part_ref, row, term[:half] + term[half:])
            return u

        u = lax.fori_loop(0, CHUNK // UNROLL, group, u)
        mixed = sum_parts(part_ref) + skip_ref[...] * x_ref[pl.ds(first, CHUNK), :]
        mixed_ref[pl.ds(first, CHUNK), :] = mixed
        out_ref[pl.ds(first, CHUNK), :] = silu(mixed).astype(bf16)
        return u

    lax.fori_loop(0, length // CHUNK, chunk, jnp.zeros((states, width), f32))


def ema_forward(alive, source, keep, blend, skip):
    length, channels = source.shape
    states = keep.shape[0]
    whole = lambda rows: pl.BlockSpec((rows, channels), lambda i: (0, 0))
    return pl.pallas_call(
        ema_forward_kernel,
        grid=(1,),
        in_specs=[
            pl.BlockSpec(memory_space=pltpu.SMEM),
            whole(length),
            whole(states),
            whole(states),
            whole(1),
        ],
        out_specs=[whole(length), whole(length)],
        out_shape=[
            jax.ShapeDtypeStruct((length, channels), f32),
            jax.ShapeDtypeStruct((length, channels), bf16),
        ],
        scratch_shapes=[pltpu.VMEM((channels // 128, CHUNK * 8, 128), f32)],
        compiler_params=pltpu.CompilerParams(vmem_limit_bytes=40 << 20),
        cost_estimate=pl.CostEstimate(
            flops=6 * length * channels * states,
            bytes_accessed=40 << 20,
            transcendentals=length * channels,
        ),
        name="ema_forward",
    )(alive, source, keep, blend, skip)


def ema_backward_kernel(
    alive_ref, x_ref, dm_ref, keep_ref, blend_ref, skip_ref, ds_ref, b_ref, g_ref, k_ref, part_ref
):
    states, width = keep_ref.shape
    length = x_ref.shape[0]
    keep = keep_ref[...]
    blend = blend_ref[...]
    half = states // 2

    def chunk(index, carry):
        first = pl.multiple_of(index * CHUNK, CHUNK)
        back = pl.multiple_of(length - CHUNK - index * CHUNK, CHUNK)

        def group(group_index, carry):
            u, w, v, b_sum, g_sum = carry
            for step in range(UNROLL):
                row = group_index * UNROLL + step
                token = first + row
                alive = alive_ref[token]
                dm = dm_ref[pl.ds(token, 1), :]
                kept = alive * u
                w = keep * (alive * w) + kept
                u = keep * kept + x_ref[pl.ds(token, 1), :]
                b_sum = b_sum + dm * u
                g_sum = g_sum + dm * w
                row_back = CHUNK - 1 - row
                token_back = back + row_back
                v = dm_ref[pl.ds(token_back, 1), :] + (keep * alive_ref[token_back + 1]) * v
                term = v * blend
                store_part(part_ref, row_back, term[:half] + term[half:])
            return u, w, v, b_sum, g_sum

        carry = lax.fori_loop(0, CHUNK // UNROLL, group, carry)
        ds_ref[pl.ds(back, CHUNK), :] = (
            sum_parts(part_ref) + skip_ref[...] * dm_ref[pl.ds(back, CHUNK), :]
        )
        return carry

    zero = jnp.zeros((states, width), f32)
    _, _, _, b_sum, g_sum = lax.fori_loop(0, length // CHUNK, chunk, (zero,) * 5)
    b_ref[...] = b_sum
    g_ref[...] = g_sum
    k_ref[...] = jnp.sum(x_ref[...] * dm_ref[...], axis=0, keepdims=True)


def ema_backward(alive, source, d_mixed, keep, blend, skip):
    length, channels = source.shape
    states = keep.shape[0]
    width = min(256, channels)
    block = lambda rows: pl.BlockSpec((rows, width), lambda i: (0, i))
    return pl.pallas_call(
        ema_backward_kernel,
        grid=(channels // width,),
        in_specs=[
            pl.BlockSpec(memory_space=pltpu.SMEM),
            block(length),
            block(length),
            block(states),
            block(states),
            block(1),
        ],
        out_specs=[block(length), block(states), block(states), block(1)],
        out_shape=[
            jax.ShapeDtypeStruct((length, channels), f32),
            jax.ShapeDtypeStruct((states, channels), f32),
            jax.ShapeDtypeStruct((states, channels), f32),
            jax.ShapeDtypeStruct((1, channels), f32),
        ],
        scratch_shapes=[pltpu.VMEM((width // 128, CHUNK * 8, 128), f32)],
        compiler_params=pltpu.CompilerParams(vmem_limit_bytes=40 << 20),
        cost_estimate=pl.CostEstimate(
            flops=15 * length * channels * states, bytes_accessed=80 << 20, transcendentals=0
        ),
        name="ema_backward",
    )(alive, source, d_mixed, keep, blend, skip)


def core_swap(values):
    return lax.ppermute(values, "tensor", [(0, 1), (1, 0), (2, 3), (3, 2)])


def y_swap(values):
    return lax.ppermute(values, "tensor", [(0, 2), (2, 0), (1, 3), (3, 1)])


def dp_swap(values, dp, mask):
    return lax.ppermute(values, "dp", [(i, i ^ mask) for i in range(dp)])


def pick(values, index, axis=0):
    return lax.dynamic_index_in_dim(values, index, axis, keepdims=False)


def ordered(flag, first, second, axis):
    return jnp.concatenate(
        [jnp.where(flag, first, second), jnp.where(flag, second, first)], axis=axis
    )


def dp_scatter(values, dp, place, link):
    line = dp // 2
    if line > 4 or dp % 2:
        return pick(lax.psum_scatter(values, "dp", scatter_dimension=0, tiled=True), 0).astype(f32)
    x = place % 2
    z = place // 2
    pairs = values.reshape((line, 2) + values.shape[1:])
    sums = pick(pairs, x, 1).astype(f32) + dp_swap(pick(pairs, 1 - x, 1).astype(link), dp, 1).astype(f32)
    total = pick(sums, z)
    for up in (True, False):
        position = z if up else line - 1 - z
        arrived = None
        for step in range(1, line):
            aim = jnp.minimum(position + line - step, line - 1)
            message = pick(sums, aim if up else line - 1 - aim)
            if arrived is not None:
                message = message + arrived
            chain = []
            for p in range(min(step, line - 1)):
                source, target = (p, p + 1) if up else (line - 1 - p, line - 2 - p)
                chain += [(2 * source, 2 * target), (2 * source + 1, 2 * target + 1)]
            arrived = lax.ppermute(message.astype(link), "dp", chain).astype(f32)
        if arrived is not None:
            total = total + arrived
    return total


def sum_everywhere(values, dp):
    values = values + core_swap(values)
    values = values + y_swap(values)
    mask = 1
    while mask < dp:
        values = values + dp_swap(values, dp, mask)
        mask *= 2
    return values


def on_device(
    block_input,
    segment_ids,
    pad_mask,
    norm_gain,
    ema_forget,
    ema_mix,
    ema_skip,
    proj_shared,
    query_gain,
    query_bias,
    key_gain,
    proj_value,
    proj_reset,
    proj_out,
    ffn_gain,
    ffn_up,
    ffn_down,
    cotangent,
    *,
    dp,
):
    shard = lax.axis_index("tensor")
    place = lax.axis_index("dp")
    y = shard // 2
    c = shard % 2
    x = place % 2
    is_first_y = y == 0
    is_first_c = c == 0
    length, model_width = block_input.shape[1:]
    zdim = proj_shared.shape[1]
    channels, states = ema_forget.shape
    quarter = cotangent.shape[1]
    half_rows = 2 * quarter
    own_cols = proj_value.shape[1]

    def fetch(weight):
        halves = weight.reshape((2, weight.shape[0] // 2) + weight.shape[1:])
        direct = y_swap(pick(halves, x))
        around = dp_swap(direct, dp, 1)
        return ordered(x == 0, direct, around, 0)

    def by_rows(values):
        width = values.shape[1]
        split = values.reshape(2, 2, quarter, width)
        return (
            pick(split, c, 1).reshape(half_rows, width),
            pick(split, 1 - c, 1).reshape(half_rows, width),
        )

    def all_rows(mine, theirs):
        width = mine.shape[1]
        mine = mine.reshape(2, 1, quarter, width)
        theirs = theirs.reshape(2, 1, quarter, width)
        return ordered(is_first_c, mine, theirs, 1).reshape(length, width)

    def all_channels(mine, theirs):
        rows = mine.shape[0]
        mine = mine.reshape(rows, 2, 1, channels)
        theirs = theirs.reshape(rows, 2, 1, channels)
        return ordered(is_first_c, mine, theirs, 2).reshape(rows, model_width)

    def my_channels(values, core, axis):
        split = values.reshape(
            values.shape[:axis] + (2, 2, channels) + values.shape[axis + 1 :]
        )
        chosen = pick(split, core, axis + 1)
        return chosen.reshape(values.shape[:axis] + (2 * channels,) + values.shape[axis + 1 :])

    own_params = jnp.concatenate([ema_forget.T, ema_mix.T, ema_skip[None]], axis=0)
    params = ordered(is_first_y, own_params, y_swap(own_params), 1)
    forget = params[:states]
    mix = params[states : 2 * states]
    skip = params[2 * states :]
    keep = 1.0 - forget
    blend = forget * mix

    weight_value = jnp.concatenate([proj_value, fetch(proj_value)], axis=1)
    weight_reset = jnp.concatenate([proj_reset, fetch(proj_reset)], axis=1)
    weight_out = jnp.concatenate([proj_out, fetch(proj_out)], axis=0)

    inputs = pick(block_input, y).astype(f32)
    segments = pick(segment_ids, y)
    padding = pick(pad_mask, y)
    alive = jnp.concatenate(
        [jnp.zeros((1,), f32), (segments[1:] == segments[:-1]).astype(f32), jnp.zeros((1,), f32)]
    )
    pad_float = padding.astype(f32)[:, None]
    normed = rms_norm(inputs, norm_gain).astype(bf16)
    source = my_channels(normed, c, 1).astype(f32) * pad_float
    mixed, ema_mine = ema_forward(alive, source, keep, blend, skip)
    ema_all = all_channels(ema_mine, core_swap(ema_mine))

    pre_shared = matmul(ema_all, proj_shared)
    shared = silu(pre_shared)
    query = (shared * query_gain + query_bias).astype(bf16)
    key = (shared * key_gain).astype(bf16)
    pre_value = matmul(normed, weight_value)
    values = silu(pre_value).astype(bf16)
    pre_reset = matmul(ema_all, weight_reset)
    reset = silu(pre_reset)

    places = jnp.arange(length, dtype=jnp.int32)
    allowed = (segments[:, None] == segments[None, :]) & (
        (padding[None, :] > 0) | (places[:, None] == places[None, :])
    )
    score_scale = zdim ** (-0.5)
    scores = jnp.where(allowed, inner_cols(query, key) * score_scale, -1000000000.0)
    prob_full = jax.nn.softmax(scores, axis=-1)
    prob = prob_full.astype(bf16)
    attn = matmul(prob, values)
    heard = (attn * reset).astype(bf16)

    part_mine, part_theirs = by_rows(matmul(heard, weight_out).astype(bf16))
    attn_rows = part_mine.astype(f32) + core_swap(part_theirs).astype(f32)
    input_rows, _ = by_rows(inputs)
    middle_rows = input_rows + attn_rows
    normed_rows, norm_two_back = jax.vjp(rms_norm, middle_rows, ffn_gain)
    normed_rows = normed_rows.astype(bf16)

    cot_far = y_swap(cotangent)
    cot_mine = ordered(is_first_y, cotangent[:, None], cot_far[:, None], 1).reshape(
        2, half_rows, model_width
    )
    cot_theirs = core_swap(cot_mine)
    cot_own = jnp.concatenate([pick(cot_mine, y), pick(cot_theirs, y)], axis=0)
    cot_other = jnp.concatenate([pick(cot_mine, 1 - y), pick(cot_theirs, 1 - y)], axis=0)

    normed_far = y_swap(normed_rows)
    two_own = jnp.concatenate([normed_rows, core_swap(normed_rows)], axis=0)
    two_other = jnp.concatenate([normed_far, core_swap(normed_far)], axis=0)

    def ffn(two, cot):
        d_hidden = inner_cols(cot, ffn_down)
        pre_up = matmul(two, ffn_up)
        hidden = silu(pre_up).astype(bf16)
        d_pre_up = (d_hidden * silu_slope(pre_up)).astype(bf16)
        d_two = inner_cols(d_pre_up, ffn_up).astype(bf16)
        result = matmul(hidden, ffn_down).astype(bf16)
        return hidden, d_pre_up, d_two, result

    hidden_own, d_pre_own, d_two_own, result_own = ffn(two_own, cot_own)
    hidden_other, d_pre_other, d_two_other, result_other = ffn(two_other, cot_other)

    def collect(own, other):
        chip_other = other[:half_rows].astype(f32) + core_swap(other[half_rows:]).astype(f32)
        far = y_swap(chip_other.astype(bf16))
        near = own[:half_rows].astype(f32) + core_swap(own[half_rows:]).astype(f32)
        return near + far.astype(f32)

    def place_rows(rows):
        slots = rows.astype(bf16).reshape(2, quarter, model_width)
        kept = pick(slots, y)
        arrived = y_swap(pick(slots, 1 - y))
        return ordered(is_first_y, kept[None], arrived[None], 0)

    d_two_rows = collect(d_two_own, d_two_other)
    d_middle_part, g_ffn_gain = norm_two_back(d_two_rows)
    d_middle_rows = pick(cot_mine, y).astype(f32) + d_middle_part
    d_middle_low = d_middle_rows.astype(bf16)
    d_middle = all_rows(d_middle_low, core_swap(d_middle_low))

    block_output = place_rows(middle_rows + collect(result_own, result_other))
    g_down = (inner_rows(hidden_own, cot_own) + inner_rows(hidden_other, cot_other)).astype(bf16)
    g_up = (inner_rows(two_own, d_pre_own) + inner_rows(two_other, d_pre_other)).astype(bf16)
    per_dp = lambda grad: grad.reshape((dp, grad.shape[0] // dp) + grad.shape[1:])
    grad_down = dp_scatter(per_dp(g_down), dp, place, bf16)
    grad_up = dp_scatter(per_dp(g_up), dp, place, bf16)

    d_heard = inner_cols(d_middle, weight_out)
    g_out = inner_rows(heard, d_middle).astype(bf16)
    d_attn = (d_heard * reset).astype(bf16)
    d_pre_reset = (d_heard * attn * silu_slope(pre_reset)).astype(bf16)
    d_prob = inner_cols(d_attn, values)
    row_inner = jnp.sum(prob_full * d_prob, axis=1, keepdims=True)
    d_scores = (prob_full * (d_prob - row_inner)).astype(bf16)
    d_query_key = jnp.concatenate(
        [matmul(d_scores, key) * score_scale, inner_rows(d_scores, query) * score_scale], axis=1
    )
    d_query_key = d_query_key + core_swap(d_query_key.astype(bf16)).astype(f32)
    d_query = d_query_key[:, :zdim]
    d_key = d_query_key[:, zdim:]
    d_values = inner_rows(prob, d_attn)
    d_pre_value = (d_values * silu_slope(pre_value)).astype(bf16)

    g_reset = inner_rows(ema_all, d_pre_reset).astype(bf16)
    g_value = inner_rows(normed, d_pre_value).astype(bf16)

    def chip_pair(own, other):
        return own.astype(f32) + y_swap(other).astype(f32)

    grad_out = dp_scatter(per_dp(chip_pair(g_out[:own_cols], g_out[own_cols:])), dp, place, bf16)
    grad_reset = dp_scatter(
        per_dp(chip_pair(g_reset[:, :own_cols], g_reset[:, own_cols:])), dp, place, bf16
    )
    grad_value = dp_scatter(
        per_dp(chip_pair(g_value[:, :own_cols], g_value[:, own_cols:])), dp, place, bf16
    )

    d_shared = d_query * query_gain + d_key * key_gain
    d_pre_shared = (d_shared * silu_slope(pre_shared)).astype(bf16)
    g_shared = inner_rows(ema_mine, d_pre_shared)
    d_ema_theirs = inner_cols(d_pre_reset, my_channels(weight_reset, 1 - c, 0)).astype(bf16)
    d_ema = (
        inner_cols(d_pre_shared, my_channels(proj_shared, c, 0))
        + inner_cols(d_pre_reset, my_channels(weight_reset, c, 0))
        + core_swap(d_ema_theirs).astype(f32)
    )
    d_mixed = d_ema * silu_slope(mixed)
    d_source, b_sum, g_sum, g_skip = ema_backward(alive, source, d_mixed, keep, blend, skip)
    d_source = d_source * pad_float

    normed_mine, normed_theirs = by_rows(inner_cols(d_pre_value, weight_value).astype(bf16))
    source_mine, source_theirs = by_rows(d_source)
    d_normed = (
        normed_mine.astype(f32)
        + core_swap(normed_theirs).astype(f32)
        + all_channels(source_mine, core_swap(source_theirs.astype(bf16)).astype(f32))
    )
    _, norm_one_back = jax.vjp(rms_norm, input_rows, norm_gain)
    d_input_part, g_norm_gain = norm_one_back(d_normed)
    grad_input = place_rows(d_middle_rows + d_input_part)

    g_forget = mix * (b_sum - forget * g_sum)
    g_mix = forget * b_sum
    by_channel = jnp.concatenate([g_shared, g_forget.T, g_mix.T, g_skip.T], axis=1)
    by_channel = by_channel.reshape(2, channels, by_channel.shape[1])
    by_channel = pick(by_channel, y) + y_swap(pick(by_channel, 1 - y))
    by_channel = dp_scatter(per_dp(by_channel), dp, place, f32)
    grad_shared = by_channel[:, :zdim]
    grad_forget = by_channel[:, zdim : zdim + states]
    grad_mix = by_channel[:, zdim + states : zdim + 2 * states]
    grad_skip = by_channel[:, zdim + 2 * states]

    leader = is_first_c.astype(f32)
    light = jnp.concatenate(
        [
            g_norm_gain,
            g_ffn_gain,
            jnp.sum(d_query * shared, axis=0) * leader,
            jnp.sum(d_query, axis=0) * leader,
            jnp.sum(d_key * shared, axis=0) * leader,
        ]
    )
    light = sum_everywhere(light, dp)
    cuts = [model_width, 2 * model_width, 2 * model_width + zdim, 2 * model_width + 2 * zdim]
    grad_norm_gain, grad_ffn_gain, grad_query_gain, grad_query_bias, grad_key_gain = jnp.split(
        light, cuts
    )
    return (
        block_output,
        grad_input,
        grad_norm_gain,
        grad_forget,
        grad_mix,
        grad_skip,
        grad_shared,
        grad_query_gain,
        grad_query_bias,
        grad_key_gain,
        grad_value,
        grad_reset,
        grad_out,
        grad_ffn_gain,
        grad_up,
        grad_down,
    )


def solution(mesh):
    in_specs = (
        P("dp", None, None),
        P("dp", None),
        P("dp", None),
        P(),
        P("tensor", None),
        P("tensor", None),
        P("tensor"),
        P(),
        P(),
        P(),
        P(),
        P(None, "tensor"),
        P(None, "tensor"),
        P("tensor", None),
        P(),
        P(None, "tensor"),
        P("tensor", None),
        P("dp", "tensor", None),
    )
    out_specs = (
        P("dp", "tensor", None),
        P("dp", "tensor", None),
        P(),
        P(("tensor", "dp"), None),
        P(("tensor", "dp"), None),
        P(("tensor", "dp")),
        P(("tensor", "dp"), None),
        P(),
        P(),
        P(),
        P("dp", "tensor"),
        P("dp", "tensor"),
        P(("tensor", "dp"), None),
        P(),
        P("dp", "tensor"),
        P(("tensor", "dp"), None),
    )
    return jax.shard_map(
        functools.partial(on_device, dp=mesh.shape["dp"]),
        mesh=mesh,
        in_specs=in_specs,
        out_specs=out_specs,
        check_vma=False,
    )
```

```python
import functools

import jax
import jax.numpy as jnp
from jax import lax
from jax.experimental import pallas as pl
from jax.experimental.pallas import tpu as pltpu
from jax.sharding import PartitionSpec as P

epsilon = 1e-06
dims_rows = (((0,), (0,)), ((), ()))
dims_cols = (((1,), (1,)), ((), ()))
f32 = jnp.float32
bf16 = jnp.bfloat16

CHUNK = 64
UNROLL = 8


def cost(microseconds):
    return pl.CostEstimate(flops=0, bytes_accessed=int(1.7e6 * microseconds), transcendentals=0)


def rms_norm(values, gain):
    return values * lax.rsqrt(jnp.mean(values * values, axis=-1, keepdims=True) + epsilon) * gain


def silu(values):
    return values * jax.nn.sigmoid(values)


def silu_slope(values):
    sigma = jax.nn.sigmoid(values)
    return sigma * (1.0 + values * (1.0 - sigma))


def matmul(left, right):
    return jnp.dot(left, right, preferred_element_type=f32)


def inner_rows(left, right):
    return lax.dot_general(left, right, dims_rows, preferred_element_type=f32)


def inner_cols(left, right):
    return lax.dot_general(left, right, dims_cols, preferred_element_type=f32)


def store_part(part_ref, row, values):
    for lane_group in range(part_ref.shape[0]):
        part_ref[lane_group, pl.ds(pl.multiple_of(row * 8, 8), 8), :] = values[
            :, lane_group * 128 : (lane_group + 1) * 128
        ]


def sum_parts(part_ref):
    columns = []
    for lane_group in range(part_ref.shape[0]):
        total = part_ref[lane_group, pl.ds(0, CHUNK, stride=8), :]
        for sub in range(1, 8):
            total = total + part_ref[lane_group, pl.ds(sub, CHUNK, stride=8), :]
        columns.append(total)
    return jnp.concatenate(columns, axis=1)


def ema_forward_kernel(
    alive_ref, x_ref, keep_ref, blend_ref, skip_ref, mixed_ref, out_ref, tok_ref, part_ref
):
    states, width = keep_ref.shape
    length = x_ref.shape[0]
    keep = keep_ref[...]
    blend = blend_ref[...]
    half = states // 2
    tok_ref[0, 0] = 0.0

    def chunk(index, u):
        first = pl.multiple_of(index * CHUNK, CHUNK)

        def group(group_index, u):
            for step in range(UNROLL):
                row = group_index * UNROLL + step
                token = first + row
                u = (keep * alive_ref[token]) * u + x_ref[pl.ds(token, 1), :]
                term = u * blend
                store_part(part_ref, row, term[:half] + term[half:])
            return u

        u = lax.fori_loop(0, CHUNK // UNROLL, group, u)
        mixed = sum_parts(part_ref) + skip_ref[...] * x_ref[pl.ds(first, CHUNK), :]
        mixed_ref[pl.ds(first, CHUNK), :] = mixed
        out_ref[pl.ds(first, CHUNK), :] = silu(mixed).astype(bf16)
        return u

    lax.fori_loop(0, length // CHUNK, chunk, jnp.zeros((states, width), f32))


def ema_forward(alive, source, keep, blend, skip, group, hold, mixed=None):
    length = source.shape[0]
    states = keep.shape[0]
    channels = source.shape[1] // 2
    at = lambda rows: pl.BlockSpec((rows, channels), lambda i: (0, group))
    whole = pl.BlockSpec((length, channels), lambda i: (0, 0))
    smem = pl.BlockSpec(memory_space=pltpu.SMEM)
    count = 5
    hold = (() if mixed is None else (mixed,)) + tuple(hold)

    def body(*refs):
        ema_forward_kernel(*refs[:count], *refs[count + len(hold) :])

    return pl.pallas_call(
        body,
        grid=(1,),
        in_specs=[smem, at(length), at(states), at(states), at(1)]
        + [pl.BlockSpec(memory_space=pl.ANY)] * len(hold),
        out_specs=[at(length), whole, smem],
        out_shape=[
            jax.ShapeDtypeStruct((length, 2 * channels), f32),
            jax.ShapeDtypeStruct((length, channels), bf16),
            jax.ShapeDtypeStruct((1, 1), f32),
        ],
        scratch_shapes=[pltpu.VMEM((channels // 128, CHUNK * 8, 128), f32)],
        input_output_aliases={} if mixed is None else {count: 0},
        compiler_params=pltpu.CompilerParams(vmem_limit_bytes=12 << 20),
        cost_estimate=cost(6.3),
        name="ema_forward",
    )(alive, source, keep, blend, skip, *hold)


def ema_source_kernel(alive_ref, dm_ref, keep_ref, blend_ref, skip_ref, ds_ref, tok_ref, part_ref):
    states, width = keep_ref.shape
    length = dm_ref.shape[0]
    keep = keep_ref[...]
    blend = blend_ref[...]
    half = states // 2
    tok_ref[0, 0] = 0.0

    def chunk(index, v):
        back = pl.multiple_of(length - CHUNK - index * CHUNK, CHUNK)

        def group(group_index, v):
            for step in range(UNROLL):
                row = CHUNK - 1 - (group_index * UNROLL + step)
                token = back + row
                v = dm_ref[pl.ds(token, 1), :] + (keep * alive_ref[token + 1]) * v
                term = v * blend
                store_part(part_ref, row, term[:half] + term[half:])
            return v

        v = lax.fori_loop(0, CHUNK // UNROLL, group, v)
        ds_ref[pl.ds(back, CHUNK), :] = (
            sum_parts(part_ref) + skip_ref[...] * dm_ref[pl.ds(back, CHUNK), :]
        )
        return v

    lax.fori_loop(0, length // CHUNK, chunk, jnp.zeros((states, width), f32))


def ema_source(alive, d_mixed, keep, blend, skip, hold):
    length, channels = d_mixed.shape
    states = keep.shape[0]
    whole = lambda rows: pl.BlockSpec((rows, channels), lambda i: (0, 0))
    smem = pl.BlockSpec(memory_space=pltpu.SMEM)
    count = 5

    def body(*refs):
        ema_source_kernel(*refs[:count], *refs[count + len(hold) :])

    return pl.pallas_call(
        body,
        grid=(1,),
        in_specs=[smem, whole(length), whole(states), whole(states), whole(1)]
        + [pl.BlockSpec(memory_space=pl.ANY)] * len(hold),
        out_specs=[whole(length), smem],
        out_shape=[
            jax.ShapeDtypeStruct((length, channels), f32),
            jax.ShapeDtypeStruct((1, 1), f32),
        ],
        scratch_shapes=[pltpu.VMEM((channels // 128, CHUNK * 8, 128), f32)],
        compiler_params=pltpu.CompilerParams(vmem_limit_bytes=16 << 20),
        cost_estimate=cost(10.0),
        name="ema_source",
    )(alive, d_mixed, keep, blend, skip, *hold)


def ema_rates_kernel(alive_ref, x_ref, dm_ref, keep_ref, b_ref, g_ref, k_ref, tok_ref):
    states, width = keep_ref.shape
    length = x_ref.shape[0]
    keep = keep_ref[...]
    tok_ref[0, 0] = 0.0

    def group(group_index, carry):
        u, w, b_sum, g_sum = carry
        for step in range(UNROLL):
            token = group_index * UNROLL + step
            alive = alive_ref[token]
            dm = dm_ref[pl.ds(token, 1), :]
            kept = alive * u
            w = keep * (alive * w) + kept
            u = keep * kept + x_ref[pl.ds(token, 1), :]
            b_sum = b_sum + dm * u
            g_sum = g_sum + dm * w
        return u, w, b_sum, g_sum

    zero = jnp.zeros((states, width), f32)
    _, _, b_sum, g_sum = lax.fori_loop(0, length // UNROLL, group, (zero,) * 4)
    b_ref[...] = b_sum
    g_ref[...] = g_sum
    k_ref[...] = jnp.sum(x_ref[...] * dm_ref[...], axis=0, keepdims=True)


def ema_rates(alive, source, d_mixed, keep, hold):
    length, channels = source.shape
    states = keep.shape[0]
    width = min(256, channels)
    block = lambda rows: pl.BlockSpec((rows, width), lambda i: (0, i))
    smem = pl.BlockSpec(memory_space=pltpu.SMEM)
    count = 4

    def body(*refs):
        ema_rates_kernel(*refs[:count], *refs[count + len(hold) :])

    return pl.pallas_call(
        body,
        grid=(channels // width,),
        in_specs=[smem, block(length), block(length), block(states)]
        + [pl.BlockSpec(memory_space=pl.ANY)] * len(hold),
        out_specs=[block(states), block(states), block(1), smem],
        out_shape=[
            jax.ShapeDtypeStruct((states, channels), f32),
            jax.ShapeDtypeStruct((states, channels), f32),
            jax.ShapeDtypeStruct((1, channels), f32),
            jax.ShapeDtypeStruct((1, 1), f32),
        ],
        compiler_params=pltpu.CompilerParams(vmem_limit_bytes=16 << 20),
        cost_estimate=cost(14.0),
        name="ema_rates",
    )(alive, source, d_mixed, keep, *hold)


TILE = 256


def tile_call(kernel, steps, spot, ins, outs, scratch, microseconds, name, mib, hold=()):
    smem = pl.BlockSpec(memory_space=pltpu.SMEM)
    count = len(ins)

    def body(spot_ref, *refs):
        rest = refs[count + len(hold) :]
        rest[len(outs)][0, 0] = 0.0
        kernel(spot_ref, *refs[:count], *rest[: len(outs)], *rest[len(outs) + 1 :])

    return pl.pallas_call(
        body,
        grid_spec=pltpu.PrefetchScalarGridSpec(
            num_scalar_prefetch=1,
            grid=(steps,),
            in_specs=[
                pl.BlockSpec(block, index, pipeline_mode=pl.Buffered(1))
                if block == v.shape
                else pl.BlockSpec(block, index)
                for v, block, index in ins
            ]
            + [pl.BlockSpec(memory_space=pl.ANY)] * len(hold),
            out_specs=[pl.BlockSpec(block, index) for _, _, block, index in outs] + [smem],
            scratch_shapes=scratch,
        ),
        out_shape=[jax.ShapeDtypeStruct(shape, dtype) for shape, dtype, _, _ in outs]
        + [jax.ShapeDtypeStruct((1, 1), f32)],
        compiler_params=pltpu.CompilerParams(vmem_limit_bytes=mib << 20),
        cost_estimate=cost(microseconds),
        name=name,
    )(spot, *[v for v, _, _ in ins], *hold)


def whole_map(rank):
    return lambda i, s: (0,) * rank


def row_map(i, s):
    return (i, 0)


def slot_map(i, s):
    return (i // 2, 0, 0)


def norm_factor(values):
    return lax.rsqrt(jnp.mean(values * values, axis=-1, keepdims=True) + epsilon)


def by_core(c, groups):
    first = c == 0
    g0, g1, g2, g3 = groups
    mine = jnp.concatenate([jnp.where(first, g0, g1), jnp.where(first, g2, g3)], axis=1)
    theirs = jnp.concatenate([jnp.where(first, g1, g0), jnp.where(first, g3, g2)], axis=1)
    return mine, theirs


def lane_groups(values):
    width = values.shape[1] // 4
    return [values[:, k * width : (k + 1) * width] for k in range(4)]


def first_norm_kernel(spot, in_ref, gain_ref, normed_ref, source_ref, rows_ref):
    low = in_ref[0]
    values = low.astype(f32)

    @pl.when(lax.rem(pl.program_id(0), 2) == spot[1])
    def _():
        rows_ref[0] = low

    normed = (values * norm_factor(values) * gain_ref[...]).astype(bf16)
    normed_ref[...] = normed
    mine, _ = by_core(spot[1], lane_groups(normed.astype(f32)))
    rows = pl.program_id(0) * TILE + lax.broadcasted_iota(jnp.int32, mine.shape, 0)
    source_ref[...] = jnp.where(rows < spot[2], mine, 0.0)


def first_norm(spot, block_input, gain):
    _, length, width = block_input.shape
    return tile_call(
        first_norm_kernel,
        length // TILE,
        spot,
        [
            (block_input, (1, TILE, width), lambda i, s: (s[0], i, 0)),
            (gain[None], (1, width), whole_map(2)),
        ],
        [
            ((length, width), bf16, (TILE, width), row_map),
            ((length, width // 2), f32, (TILE, width // 2), row_map),
            ((2, TILE, width), bf16, (1, TILE, width), slot_map),
        ],
        [],
        2.5,
        "first_norm",
        12,
    )


def masked_scores(q, key, seg_rows, seg_cols, first_row):
    scores = inner_cols(q, key) * (q.shape[1] ** (-0.5))
    rows = first_row + lax.broadcasted_iota(jnp.int32, scores.shape, 0)
    cols = lax.broadcasted_iota(jnp.int32, scores.shape, 1)
    return jnp.where((seg_rows == seg_cols) | (rows == cols), scores, -1000000000.0)


def attend_kernel(
    spot, q_ref, k_ref, segr_ref, segc_ref, va_ref, vb_ref, ra_ref, rb_ref,
    attn_ref, heard_ref, lse_ref,
):
    step = pl.program_id(0)
    scores = masked_scores(q_ref[...], k_ref[...], segr_ref[...], segc_ref[...], step * TILE)
    top = jnp.max(scores, axis=1, keepdims=True)
    grown = jnp.exp(scores - top)
    total = jnp.sum(grown, axis=1, keepdims=True)
    prob = (grown * (1.0 / total)).astype(bf16)
    lse_ref[...] = top + jnp.log(total)
    cols = va_ref.shape[1]
    for side, (v_ref, r_ref) in enumerate(((va_ref, ra_ref), (vb_ref, rb_ref))):
        here = slice(side * cols, (side + 1) * cols)
        attn = matmul(prob, v_ref[...])
        attn_ref[:, here] = attn.astype(bf16)
        heard_ref[:, here] = (attn * silu(r_ref[...].astype(f32))).astype(bf16)


def attend(spot, query, key, seg_rows, seg_cols, values, resets):
    length, zdim = query.shape
    cols = values[0].shape[1]
    tile = lambda v: (v, (TILE, v.shape[1]), row_map)
    whole = lambda v: (v, v.shape, whole_map(2))
    out = ((length, 2 * cols), bf16, (TILE, 2 * cols), row_map)
    return tile_call(
        attend_kernel,
        length // TILE,
        spot,
        [tile(query), whole(key), tile(seg_rows), whole(seg_cols)]
        + [whole(v) for v in values]
        + [tile(r) for r in resets],
        [out] * 2 + [((length, 1), f32, (TILE, 1), row_map)],
        [],
        6.2,
        "attend",
        24,
    )


def out_kernel(spot, heard_ref, wa_ref, wb_ref, mine_ref, theirs_ref):
    depth = wa_ref.shape[0]
    result = matmul(heard_ref[:, :depth], wa_ref[...]) + matmul(heard_ref[:, depth:], wb_ref[...])
    is_mine = lax.rem(pl.program_id(0), 2) == spot[1]

    @pl.when(is_mine)
    def _():
        mine_ref[0] = result.astype(bf16)

    @pl.when(jnp.logical_not(is_mine))
    def _():
        theirs_ref[0] = result.astype(bf16)


def out_rows(spot, heard, weights):
    length, depth = heard.shape
    width = weights[0].shape[1]
    side = ((2, TILE, width), bf16, (1, TILE, width), slot_map)
    return tile_call(
        out_kernel,
        length // TILE,
        spot,
        [(heard, (TILE, depth), row_map)] + [(w, w.shape, whole_map(2)) for w in weights],
        [side, side],
        [],
        4.5,
        "out_rows",
        16,
    )


def attend_back_kernel(
    spot, dm_ref, q_ref, k_ref, segr_ref, segc_ref, lse_ref, a_ref,
    woa_ref, wob_ref, va_ref, vb_ref, pva_ref, pvb_ref, wra_ref, wrb_ref, pra_ref, prb_ref,
    dpr_ref, dpv_ref, dq_ref, dk_ref, mine_ref, theirs_ref,
    dva_ref, dvb_ref,
):
    step = pl.program_id(0)
    cols = va_ref.shape[1]
    scale = q_ref.shape[1] ** (-0.5)
    scores = masked_scores(q_ref[...], k_ref[...], segr_ref[...], segc_ref[...], step * TILE)
    prob = jnp.exp(scores - lse_ref[...])
    prob_low = prob.astype(bf16)
    d_middle = dm_ref[...]
    d_prob = None
    d_ema = None

    @pl.when(step == 0)
    def _():
        dk_ref[...] = jnp.zeros_like(dk_ref)
        dva_ref[...] = jnp.zeros_like(dva_ref)
        dvb_ref[...] = jnp.zeros_like(dvb_ref)

    for side, (wo_ref, v_ref, wr_ref, pr_ref, dv_ref) in enumerate(
        ((woa_ref, va_ref, wra_ref, pra_ref, dva_ref), (wob_ref, vb_ref, wrb_ref, prb_ref, dvb_ref))
    ):
        here = slice(side * cols, (side + 1) * cols)
        d_heard = inner_cols(d_middle, wo_ref[...])
        pre = pr_ref[...].astype(f32)
        sigma = jax.nn.sigmoid(pre)
        d_attn = (d_heard * (pre * sigma)).astype(bf16)
        slope = sigma * (1.0 + pre * (1.0 - sigma))
        d_reset = (d_heard * a_ref[:, here].astype(f32) * slope).astype(bf16)
        dpr_ref[:, here] = d_reset
        part = inner_cols(d_attn, v_ref[...])
        d_prob = part if d_prob is None else d_prob + part
        dv_ref[...] += inner_rows(prob_low, d_attn)
        part = inner_cols(d_reset, wr_ref[...])
        d_ema = part if d_ema is None else d_ema + part
    mine, theirs = by_core(spot[1], lane_groups(d_ema))
    mine_ref[...] = mine
    theirs_ref[...] = theirs.astype(bf16)
    inner = jnp.sum(prob * d_prob, axis=1, keepdims=True)
    d_scores = (prob * (d_prob - inner)).astype(bf16)
    dq_ref[...] = matmul(d_scores, k_ref[...]) * scale
    dk_ref[...] += inner_rows(d_scores, q_ref[...]) * scale

    @pl.when(step == pl.num_programs(0) - 1)
    def _():
        for side, (pv_ref, dv_ref) in enumerate(((pva_ref, dva_ref), (pvb_ref, dvb_ref))):
            here = slice(side * cols, (side + 1) * cols)
            dpv_ref[:, here] = (dv_ref[...] * silu_slope(pv_ref[...].astype(f32))).astype(bf16)


def attend_back(hold, spot, d_middle, query, key, seg_rows, seg_cols, lse, attn, outs, values, pre_values, w_resets, pre_resets):
    length, zdim = query.shape
    cols = values[0].shape[1]
    width = outs[0].shape[1]
    tile = lambda v: (v, (TILE, v.shape[1]), row_map)
    whole = lambda v: (v, v.shape, whole_map(2))
    return tile_call(
        attend_back_kernel,
        length // TILE,
        spot,
        [tile(d_middle), tile(query), whole(key), tile(seg_rows), whole(seg_cols), tile(lse), tile(attn)]
        + [whole(v) for v in outs + values + pre_values + w_resets]
        + [tile(v) for v in pre_resets],
        [
            ((length, 2 * cols), bf16, (TILE, 2 * cols), row_map),
            ((length, 2 * cols), bf16, (length, 2 * cols), whole_map(2)),
            ((length, zdim), f32, (TILE, zdim), row_map),
            ((length, zdim), f32, (length, zdim), whole_map(2)),
            ((length, width // 2), f32, (TILE, width // 2), row_map),
            ((length, width // 2), bf16, (TILE, width // 2), row_map),
        ],
        [pltpu.VMEM((length, cols), f32)] * 2,
        21.0,
        "attend_back",
        36,
        hold,
    )


def second_norm_kernel(
    spot, in_ref, part_ref, got_ref, gain_ref, middle_ref, normed_ref, one_ref, two_ref
):
    middle = in_ref[0].astype(f32) + part_ref[0].astype(f32) + got_ref[0].astype(f32)
    middle_ref[0] = middle
    normed = (middle * norm_factor(middle) * gain_ref[...]).astype(bf16)
    normed_ref[0] = normed

    @pl.when(pl.program_id(0) == 0)
    def _():
        one_ref[...] = normed

    @pl.when(pl.program_id(0) > 0)
    def _():
        two_ref[...] = normed


def second_norm(spot, in_rows, part, got, gain, hold):
    slots, quarter, width = part.shape
    slot = lambda v: (v, (1, quarter, width), lambda i, s: (i, 0, 0))
    single = ((quarter, width), bf16, (quarter, width), whole_map(2))
    return tile_call(
        second_norm_kernel,
        slots,
        spot,
        [
            slot(in_rows),
            slot(part),
            slot(got),
            (gain[None], (1, width), whole_map(2)),
        ],
        [
            ((slots, quarter, width), f32, (1, quarter, width), lambda i, s: (i, 0, 0)),
            ((slots, quarter, width), bf16, (1, quarter, width), lambda i, s: (i, 0, 0)),
            single,
            single,
        ],
        [],
        3.0,
        "second_norm",
        16,
        hold,
    )


def chip_sum(spot, both, got):
    rows, width = got.shape

    def kernel(s, near_ref, got_ref, out_ref):
        out_ref[...] = (near_ref[...].astype(f32) + got_ref[...].astype(f32)).astype(bf16)

    return tile_call(
        kernel,
        1,
        spot,
        [(both, (rows, width), whole_map(2)), (got, got.shape, whole_map(2))],
        [((rows, width), bf16, (rows, width), whole_map(2))],
        [],
        1.5,
        "chip_sum",
        8,
    )


def second_norm_back_kernel(
    spot, near_ref, got_ref, far_ref, middle_ref, cot_ref, gain_ref, dm_ref, low_ref, gain_out_ref
):
    grad = near_ref[0].astype(f32) + got_ref[0].astype(f32) + far_ref[...].astype(f32)
    middle = middle_ref[0]
    factor = norm_factor(middle)
    scaled = grad * gain_ref[...]
    shift = jnp.mean(middle * scaled, axis=-1, keepdims=True) * (factor * factor * factor)
    d_middle = cot_ref[0, 0].astype(f32) + factor * scaled - middle * shift
    dm_ref[...] = d_middle
    low_ref[...] = d_middle.astype(bf16)
    part = jnp.sum(grad * middle * factor, axis=0, keepdims=True)

    @pl.when(pl.program_id(0) == 0)
    def _():
        gain_out_ref[...] = part

    @pl.when(pl.program_id(0) > 0)
    def _():
        gain_out_ref[...] += part


def second_norm_back(spot, slot, near, got, far, middle, cot, gain):
    _, quarter, width = middle.shape
    tile = quarter // 2
    pair = lambda v: (v, (1, tile, width), lambda i, s: (slot, i, 0))
    out = lambda dtype: ((quarter, width), dtype, (tile, width), row_map)
    return tile_call(
        second_norm_back_kernel,
        2,
        spot,
        [
            pair(near),
            pair(got),
            (far, (tile, width), row_map),
            pair(middle),
            (cot, (1, 1, tile, width), lambda i, s: (s[0], slot, i, 0)),
            (gain[None], (1, width), whole_map(2)),
        ],
        [out(f32), out(bf16), ((1, width), f32, (1, width), whole_map(2))],
        [],
        3.0,
        "second_norm_back",
        12,
    )


def first_norm_back_kernel(
    spot, in_ref, part_ref, got_ref, src_ref, far_ref, dm0_ref, dm1_ref, gain_ref, grad_ref,
    gain_out_ref,
):
    step = pl.program_id(0)
    quarter, half = src_ref.shape[1:]
    first = spot[1] == 0
    near = src_ref[0]
    far = far_ref[0].astype(f32)
    groups = []
    for k in range(2):
        own = near[:, k * half // 2 : (k + 1) * half // 2]
        other = far[:, k * half // 2 : (k + 1) * half // 2]
        groups += [jnp.where(first, own, other), jnp.where(first, other, own)]
    source = jnp.concatenate(groups, axis=1)
    rows = (spot[1] + 2 * step) * quarter + lax.broadcasted_iota(jnp.int32, source.shape, 0)
    source = jnp.where(rows < spot[2], source, 0.0)
    grad = part_ref[0].astype(f32) + got_ref[0].astype(f32) + source
    values = in_ref[0].astype(f32)
    factor = norm_factor(values)
    scaled = grad * gain_ref[...]
    shift = jnp.mean(values * scaled, axis=-1, keepdims=True) * (factor * factor * factor)
    d_middle = jnp.where(step == 0, dm0_ref[...], dm1_ref[...])
    grad_ref[0] = (d_middle + factor * scaled - values * shift).astype(bf16)
    part = jnp.sum(grad * values * factor, axis=0, keepdims=True)

    @pl.when(step == 0)
    def _():
        gain_out_ref[...] = part

    @pl.when(step > 0)
    def _():
        gain_out_ref[...] += part


def first_norm_back(spot, in_rows, part, got, source, source_far, d_middle, gain, hold):
    slots = 2
    quarter, width = d_middle[0].shape
    mine = lambda v: (
        v.reshape(4, quarter, v.shape[1]),
        (1, quarter, v.shape[1]),
        lambda i, s: (s[1] + 2 * i, 0, 0),
    )
    slot = lambda v, w: (v.reshape(slots, quarter, w), (1, quarter, w), lambda i, s: (i, 0, 0))
    return tile_call(
        first_norm_back_kernel,
        slots,
        spot,
        [
            slot(in_rows, width),
            mine(part),
            slot(got, width),
            mine(source),
            slot(source_far, width // 2),
            (d_middle[0], (quarter, width), whole_map(2)),
            (d_middle[1], (quarter, width), whole_map(2)),
            (gain[None], (1, width), whole_map(2)),
        ],
        [
            ((slots, quarter, width), bf16, (1, quarter, width), lambda i, s: (i, 0, 0)),
            ((1, width), f32, (1, width), whole_map(2)),
        ],
        [],
        3.0,
        "first_norm_back",
        20,
        hold,
    )


def core_swap(values):
    return lax.ppermute(values, "tensor", [(0, 1), (1, 0), (2, 3), (3, 2)])


def y_swap(values):
    return lax.ppermute(values, "tensor", [(0, 2), (2, 0), (1, 3), (3, 1)])


def dp_swap(values, dp, mask):
    return lax.ppermute(values, "dp", [(i, i ^ mask) for i in range(dp)])


def pick(values, index, axis=0):
    return lax.dynamic_index_in_dim(values, index, axis, keepdims=False)


def ordered(flag, first, second, axis):
    return jnp.concatenate(
        [jnp.where(flag, first, second), jnp.where(flag, second, first)], axis=axis
    )


def whole_in(v):
    return (v, v.shape, whole_map(v.ndim))


def whole_out(shape, dtype):
    return (shape, dtype, shape, whole_map(len(shape)))


def rows_at(number, rows):
    return pl.ds(pl.multiple_of(number * rows, rows), rows)


def add_low(left, right):
    return (left.astype(f32) + right.astype(f32)).astype(bf16)


def send_first(spot, g_reset, g_value, dp):
    line = dp // 2
    rows = g_reset.shape[0] // dp
    cols = g_reset.shape[1] // 2

    def kernel(s, reset_ref, value_ref, reset_out, value_out):
        x = lax.rem(s[3], 2)
        for h in range(line):
            at = rows_at(2 * h + 1 - x, rows)
            reset_out[0, h] = reset_ref[at, :cols]
            reset_out[1, h] = reset_ref[at, cols:]
        value_out[...] = value_ref[:, cols:]

    reset_sent, value_sent, _ = tile_call(
        kernel,
        1,
        spot,
        [whole_in(g_reset), whole_in(g_value)],
        [
            whole_out((2, line, rows, cols), bf16),
            whole_out((g_value.shape[0], cols), bf16),
        ],
        [],
        2.5,
        "send_first",
        14,
    )
    return reset_sent, value_sent


def out_second(spot, g_out, got, dp, hold):
    line = dp // 2
    rows = g_out.shape[0] // (2 * dp)
    width = g_out.shape[1]

    def kernel(s, near_ref, got_ref, sent_ref, kept_ref):
        x = lax.rem(s[3], 2)
        for h in range(line):
            for side, out_ref in ((1 - x, sent_ref), (x, kept_ref)):
                at = rows_at(2 * h + side, rows)
                out_ref[h] = add_low(near_ref[at, :], got_ref[at, :])

    out = whole_out((line, rows, width), bf16)
    sent, kept, _ = tile_call(
        kernel,
        1,
        spot,
        [(g_out, (g_out.shape[0] // 2, width), whole_map(2)), whole_in(got)],
        [out, out],
        [],
        2.5,
        "out_second",
        12,
        hold,
    )
    return sent, kept


def second_stage(spot, g_reset, reset_got, g_value, value_got, dp, hold):
    line = dp // 2
    rows = g_reset.shape[0] // dp
    cols = g_reset.shape[1] // 2

    def kernel(s, reset_ref, rgot_ref, value_ref, vgot_ref, rsent_ref, rkept_ref, vsent_ref, vkept_ref):
        x = lax.rem(s[3], 2)
        for h in range(line):
            here = rows_at(2 * h + x, rows)
            there = rows_at(2 * h + 1 - x, rows)
            rkept_ref[h] = add_low(reset_ref[here, :cols], rgot_ref[0, h])
            rsent_ref[h] = add_low(reset_ref[here, cols:], rgot_ref[1, h])
            vkept_ref[h] = add_low(value_ref[here, :cols], vgot_ref[here, :])
            vsent_ref[h] = add_low(value_ref[there, :cols], vgot_ref[there, :])

    out = whole_out((line, rows, cols), bf16)
    return tile_call(
        kernel,
        1,
        spot,
        [whole_in(v) for v in (g_reset, reset_got, g_value, value_got)],
        [out] * 4,
        [],
        4.0,
        "second_stage",
        20,
        hold,
    )


def merge_stage(spot, pairs, hold):
    (out_kept, _), (reset_kept, _), _ = pairs
    line, rows, cols = reset_kept.shape
    total_rows = rows + out_kept.shape[1]
    width = out_kept.shape[2]

    def kernel(s, ok, og, rk, rg, vk, vg, sent_ref, kept_ref):
        bit = lax.rem(lax.div(s[3], 2), 2)
        for q in range(line // 2):
            for side, out_ref in ((1 - bit, sent_ref), (bit, kept_ref)):
                h = 2 * q + side
                out_ref[q, :rows, :cols] = add_low(rk[h], rg[h])
                out_ref[q, :rows, cols:] = add_low(vk[h], vg[h])
                out_ref[q, rows:, :] = add_low(ok[h], og[h])

    out = whole_out((line // 2, total_rows, width), bf16)
    sent, kept, tok = tile_call(
        kernel,
        1,
        spot,
        [whole_in(v) for pair in pairs for v in pair],
        [out, out],
        [],
        4.0,
        "merge_stage",
        20,
        hold,
    )
    return sent, kept, tok


def line_stage(spot, kept, got, bit, hold):
    count, rows, width = kept.shape

    def kernel(s, kept_ref, got_ref, sent_ref, out_ref):
        side_here = lax.rem(lax.div(s[3], 1 << bit), 2)
        for q in range(count // 2):
            for side, ref in ((1 - side_here, sent_ref), (side_here, out_ref)):
                ref[q] = add_low(kept_ref[2 * q + side], got_ref[2 * q + side])

    out = whole_out((count // 2, rows, width), bf16)
    sent, kept, tok = tile_call(
        kernel, 1, spot, [whole_in(kept), whole_in(got)], [out, out], [], 3.0, "line_stage", 12, hold
    )
    return sent, kept, tok


def last_stage(spot, kept, got, rows, cols):
    def kernel(s, kept_ref, got_ref, out_ref, reset_ref, value_ref):
        total = lambda at, to: kept_ref[0, at, to].astype(f32) + got_ref[0, at, to].astype(f32)
        first = slice(0, rows)
        reset_ref[...] = total(first, slice(0, cols))
        value_ref[...] = total(first, slice(cols, 2 * cols))
        out_ref[...] = total(slice(rows, kept_ref.shape[1]), slice(None))

    part = whole_out((rows, cols), f32)
    return tile_call(
        kernel,
        1,
        spot,
        [whole_in(kept), whole_in(got)],
        [whole_out((kept.shape[1] - rows, kept.shape[2]), f32), part, part],
        [],
        2.0,
        "last_stage",
        8,
    )[:3]


def pack_kernel(
    spot, norm_ref, gain0_ref, gain1_ref, dq_ref, dk_ref, shared_ref, b_ref, g_ref, skip_ref,
    mix_ref, forget_ref, out_ref,
):
    width = out_ref.shape[2]
    leader = (1 - spot[1]).astype(f32)
    shared = shared_ref[...]
    total = lambda v: jnp.sum(v, axis=0, keepdims=True)
    query = jnp.concatenate([total(dq_ref[...] * shared), total(dq_ref[...])], axis=1) * leader
    key = jnp.concatenate([total(dk_ref[...] * shared)] * 2, axis=1) * leader
    gain = gain0_ref[...] + gain1_ref[...]
    parts = norm_ref.shape[1] // width
    forget = mix_ref[...] * (b_ref[...] - forget_ref[...] * g_ref[...])
    mix = forget_ref[...] * b_ref[...]
    states = forget.shape[0]
    head = out_ref.shape[1] - 2 * states
    for target in range(4):
        out_ref[target, :head, :] = jnp.zeros((head, width), f32)
        for part in range(parts):
            here = slice(part * width, (part + 1) * width)
            out_ref[target, part : part + 1, :] = norm_ref[:, here]
            out_ref[target, parts + part : parts + part + 1, :] = gain[:, here]
        out_ref[target, 2 * parts : 2 * parts + 1, :] = query
        out_ref[target, 2 * parts + 1 : 2 * parts + 2, :] = key
        here = slice((target // 2) * width, (target // 2 + 1) * width)
        mine = (spot[1] == target % 2).astype(f32)
        out_ref[target, 2 * parts + 2 : 2 * parts + 3, :] = skip_ref[:, here] * mine
        out_ref[target, head : head + states, :] = forget[:, here] * mine
        out_ref[target, head + states :, :] = mix[:, here] * mine


def pack(spot, arrays, states, channels, hold):
    head = 16
    return tile_call(
        pack_kernel,
        1,
        spot,
        [whole_in(v) for v in arrays],
        [whole_out((4, head + 2 * states, channels), f32)],
        [],
        3.0,
        "pack",
        10,
        hold,
    )[0]


def on_device(
    block_input,
    segment_ids,
    pad_mask,
    norm_gain,
    ema_forget,
    ema_mix,
    ema_skip,
    proj_shared,
    query_gain,
    query_bias,
    key_gain,
    proj_value,
    proj_reset,
    proj_out,
    ffn_gain,
    ffn_up,
    ffn_down,
    cotangent,
    *,
    dp,
):
    shard = lax.axis_index("tensor")
    place = lax.axis_index("dp")
    y = shard // 2
    c = shard % 2
    is_first_y = y == 0
    is_first_c = c == 0
    length, model_width = block_input.shape[1:]
    zdim = proj_shared.shape[1]
    channels, states = ema_forget.shape
    quarter = cotangent.shape[1]

    def fetch(weight, after=None):
        halves = weight.reshape((2, weight.shape[0] // 2) + weight.shape[1:])
        half = pick(halves, place % 2)
        if after is not None:
            half = half + after[:1, :1] * 0
        direct = y_swap(half)
        around = dp_swap(direct, dp, 1)
        return ordered(place % 2 == 0, direct, around, 0), direct, around

    def their_rows(values):
        return pick(values.reshape(2, 2, quarter, values.shape[1]), 1 - c, 1)

    def my_channels(values):
        split = values.reshape(2, 2, channels, values.shape[1])
        return pick(split, c, 1).reshape(2 * channels, values.shape[1])

    own_params = jnp.concatenate([ema_forget.T, ema_mix.T, ema_skip[None]], axis=0)
    params = ordered(is_first_y, own_params, y_swap(own_params), 1)
    forget = params[:states]
    mix = params[states : 2 * states]
    skip = params[2 * states :]
    keep = 1.0 - forget
    blend = forget * mix

    value_far, direct_value, _ = fetch(proj_value)
    reset_far, direct_reset, around_reset = fetch(proj_reset, direct_value)
    out_far, direct_out, _ = fetch(proj_out, direct_reset)
    cotangent = cotangent + (direct_out[0, 0] * 0).astype(bf16)
    cot_far = y_swap(cotangent)

    segments = pick(segment_ids, y)
    padding = pick(pad_mask, y)
    spot = jnp.stack([y, c, jnp.sum(padding), place]).astype(jnp.int32)
    alive = jnp.concatenate(
        [jnp.zeros((1,), f32), (segments[1:] == segments[:-1]).astype(f32), jnp.zeros((1,), f32)]
    )
    seg_rows = segments[:, None]
    seg_cols = jnp.where(padding > 0, segments, -1)[None]

    normed, source, in_rows, _ = first_norm(spot, block_input, norm_gain)
    mixed, ema_0, _ = ema_forward(alive, source, keep, blend, skip, 0, ())
    mixed, ema_1, _ = ema_forward(alive, source, keep, blend, skip, 1, (direct_value,), mixed)
    got_0 = core_swap(ema_0)
    got_1 = core_swap(ema_1)
    ema_all = jnp.concatenate(
        [
            jnp.where(is_first_c, ema_0, got_0),
            jnp.where(is_first_c, got_0, ema_0),
            jnp.where(is_first_c, ema_1, got_1),
            jnp.where(is_first_c, got_1, ema_1),
        ],
        axis=1,
    )

    pre_shared = matmul(ema_all, proj_shared) + around_reset[:1, :1].astype(f32) * 0.0
    shared = silu(pre_shared)
    query = (shared * query_gain + query_bias).astype(bf16)
    key = (shared * key_gain).astype(bf16)
    pre_values = [matmul(normed, w).astype(bf16) for w in (proj_value, value_far)]
    values = [silu(v.astype(f32)).astype(bf16) for v in pre_values]
    pre_resets = [matmul(ema_all, w).astype(bf16) for w in (proj_reset, reset_far)]
    attn, heard, lse, _ = attend(spot, query, key, seg_rows, seg_cols, values, pre_resets)
    out_mine, out_theirs, _ = out_rows(spot, heard, [proj_out, out_far])
    middle, normed_two, normed_0, normed_1, _ = second_norm(
        spot, in_rows, out_mine, core_swap(out_theirs), ffn_gain, (cot_far,)
    )

    cot_mine = ordered(is_first_y, cotangent[:, None], cot_far[:, None], 1)
    cot_theirs = core_swap(cot_mine)

    far_0 = y_swap(normed_0)
    far_1 = y_swap(normed_1)
    rows = lambda v: v.reshape(-1, model_width)

    def piece(two, cot):
        d_hidden = inner_cols(cot, ffn_down).astype(bf16)
        pre_up = matmul(two, ffn_up)
        hidden = silu(pre_up).astype(bf16)
        d_pre = (d_hidden.astype(f32) * silu_slope(pre_up)).astype(bf16)
        d_two = inner_cols(d_pre, ffn_up).astype(bf16)
        result = matmul(hidden, ffn_down).astype(bf16)
        return two, cot, hidden, d_pre, d_two, result

    def far_piece(far, slot, after):
        far = far + (after[0, 0] * 0).astype(bf16)
        two = jnp.concatenate([far, core_swap(far)], axis=0)
        cot = jnp.concatenate(
            [pick(cot_mine, 1 - y)[slot], pick(cot_theirs, 1 - y)[slot]], axis=0
        )
        return piece(two, cot)

    own = piece(
        jnp.concatenate([rows(normed_two), rows(core_swap(normed_two))], axis=0),
        jnp.concatenate([rows(pick(cot_mine, y)), rows(pick(cot_theirs, y))], axis=0),
    )
    far_p0 = far_piece(far_0, 0, own[4])
    far_p1 = far_piece(far_1, 1, far_p0[4])
    pieces = [own, far_p0, far_p1]

    def place_rows(rows):
        arrived = y_swap(pick(rows, 1 - y))
        return ordered(is_first_y, pick(rows, y)[None], arrived[None], 0)

    slots = lambda v: v.reshape(2, quarter, model_width)
    sum_f0, _ = chip_sum(spot, far_p0[4], core_swap(far_p0[4][quarter:]))
    sum_f1, tok_two = chip_sum(spot, far_p1[4], core_swap(far_p1[4][quarter:]))
    d_two_f0 = y_swap(sum_f0)
    d_two_f1 = y_swap(sum_f1)
    d_two_own = slots(own[4][: 2 * quarter])
    d_two_got = slots(core_swap(own[4][2 * quarter :]))
    d_mid_0, low_0, gain_0, _ = second_norm_back(
        spot, 0, d_two_own, d_two_got, d_two_f0, middle, cot_mine, ffn_gain
    )
    d_mid_1, low_1, gain_1, tok_mid = second_norm_back(
        spot, 1, d_two_own, d_two_got, d_two_f1, middle, cot_mine, ffn_gain
    )
    g_down = sum(inner_rows(hidden, cot) for _, cot, hidden, _, _, _ in pieces)
    g_down = (g_down + tok_two[0, 0]).astype(bf16)
    g_up = sum(inner_rows(two, d_pre) for two, _, _, d_pre, _, _ in pieces)
    g_up = (g_up + tok_two[0, 0]).astype(bf16)
    ffn_shares = jnp.concatenate(
        [v.reshape(dp, v.shape[0] // dp, v.shape[1]) for v in (g_down, g_up)], axis=1
    )
    grad_ffn = lax.psum_scatter(ffn_shares, "dp", scatter_dimension=0, tiled=True)[0].astype(f32)
    grad_down = grad_ffn[: g_down.shape[0] // dp]
    grad_up = grad_ffn[g_down.shape[0] // dp :]
    got_0 = core_swap(low_0)
    got_1 = core_swap(low_1)
    d_middle = jnp.concatenate(
        [
            jnp.where(is_first_c, low_0, got_0),
            jnp.where(is_first_c, got_0, low_0),
            jnp.where(is_first_c, low_1, got_1),
            jnp.where(is_first_c, got_1, low_1),
        ],
        axis=0,
    )
    own_cols = proj_value.shape[1]
    g_out = inner_rows(heard, d_middle).astype(bf16)
    out_first = g_out[own_cols:]
    out_got = y_swap(out_first)
    near_res, _ = chip_sum(spot, own[5], core_swap(own[5][2 * quarter :]))
    d_reset, d_value, d_query, d_key, d_ema_mine, d_ema_theirs, tok_back = attend_back(
        (out_first, ffn_shares, near_res),
        spot,
        d_middle,
        query,
        key,
        seg_rows,
        seg_cols,
        lse,
        attn,
        [proj_out, out_far],
        values,
        pre_values,
        [proj_reset, reset_far],
        pre_resets,
    )
    far_res = jnp.stack([slots(far_p0[5]), slots(far_p1[5])], axis=1)
    far_res = far_res[0].astype(f32) + (core_swap(far_res[1]).astype(f32) + tok_mid[0, 0])
    far_res = y_swap(far_res.astype(bf16))
    res_rows = (
        slots(near_res).astype(f32)
        + far_res.astype(f32)
        + tok_back[0, 0]
    )
    block_output = place_rows((middle + res_rows).astype(bf16))

    g_reset = inner_rows(ema_all, d_reset).astype(bf16)
    g_value = inner_rows(normed, d_value).astype(bf16)
    reset_sent, value_sent = send_first(spot, g_reset, g_value, dp)
    reset_got = dp_swap(reset_sent, dp, 1)
    value_got = y_swap(value_sent)

    d_query_key = jnp.concatenate([d_query, d_key], axis=1)
    d_query_key = d_query_key + core_swap(d_query_key.astype(bf16)).astype(f32)
    d_query = d_query_key[:, :zdim]
    d_key = d_query_key[:, zdim:]
    d_shared = d_query * query_gain + d_key * key_gain
    d_pre_shared = (d_shared * silu_slope(pre_shared)).astype(bf16)
    g_shared = jnp.stack([inner_rows(ema_0, d_pre_shared), inner_rows(ema_1, d_pre_shared)])
    g_shared = pick(g_shared, y) + y_swap(pick(g_shared, 1 - y).astype(bf16)).astype(f32)
    d_ema = (
        inner_cols(d_pre_shared, my_channels(proj_shared))
        + d_ema_mine
        + core_swap(d_ema_theirs).astype(f32)
    )
    d_mixed = d_ema * silu_slope(mixed)
    d_normed = (
        inner_cols(d_value[:, :own_cols], proj_value) + inner_cols(d_value[:, own_cols:], value_far)
    ).astype(bf16)
    d_normed_got = core_swap(their_rows(d_normed))
    d_source, tok_source = ema_source(
        alive, d_mixed, keep, blend, skip, (reset_sent, value_sent, d_normed)
    )
    out_sent, out_kept = out_second(spot, g_out, out_got, dp, (tok_source,))
    out_got = dp_swap(out_sent, dp, 1)
    b_sum, g_sum, g_skip, tok_rates = ema_rates(alive, source, d_mixed, keep, (out_sent,))
    reset_sent, reset_kept, value_sent, value_kept, _ = second_stage(
        spot, g_reset, reset_got, g_value, value_got, dp, (tok_rates,)
    )
    reset_got = y_swap(reset_sent)
    value_got = dp_swap(value_sent, dp, 1)
    grad_rows, g_norm_gain, tok_rows = first_norm_back(
        spot,
        in_rows,
        d_normed,
        d_normed_got,
        d_source,
        core_swap(their_rows(d_source).astype(bf16)),
        [d_mid_0, d_mid_1],
        norm_gain,
        (reset_sent, value_sent),
    )
    grad_input = place_rows(grad_rows)

    packed = pack(
        spot,
        (
            g_norm_gain, gain_0, gain_1, d_query, d_key, shared,
            b_sum, g_sum, g_skip, mix, forget,
        ),
        states,
        channels,
        (),
    )
    merged, kept, _ = merge_stage(
        spot,
        ((out_kept, out_got), (reset_kept, reset_got), (value_kept, value_got)),
        (packed,),
    )
    got = dp_swap(merged, dp, 2)
    for bit in range(2, dp.bit_length() - 1):
        sent, kept, _ = line_stage(spot, kept, got, bit, ())
        got = dp_swap(sent, dp, 1 << bit)
    grad_out, grad_reset, grad_value = last_stage(
        spot, kept, got, model_width // dp, own_cols
    )
    head = packed.shape[1] - 2 * states
    small = jnp.sum(lax.all_to_all(packed, "tensor", 0, 0, tiled=True), axis=0)
    share = channels // dp
    everywhere = small[:head].reshape(2 * head, zdim)
    rates = jnp.pad(small.T, ((0, 0), (0, zdim - small.shape[0])))
    pieces = [
        jnp.broadcast_to(everywhere[None], (dp,) + everywhere.shape),
        g_shared.reshape(dp, share, zdim),
        rates.reshape(dp, share, zdim),
    ]
    small = jnp.sum(
        lax.all_to_all(jnp.concatenate(pieces, axis=1), "dp", 0, 0, tiled=True), axis=0
    )
    everywhere = small[: 2 * head]
    grad_shared = small[2 * head : 2 * head + share]
    rates = small[2 * head + share :]
    grad_forget = rates[:, head : head + states]
    grad_mix = rates[:, head + states : head + 2 * states]
    grad_skip = rates[:, 2 * model_width // channels + 2]
    gains = model_width // zdim
    return (
        block_output,
        grad_input,
        everywhere[:gains].reshape(model_width),
        grad_forget,
        grad_mix,
        grad_skip,
        grad_shared,
        everywhere[2 * gains],
        everywhere[2 * gains + 1],
        everywhere[2 * gains + 2],
        grad_value,
        grad_reset,
        grad_out,
        everywhere[gains : 2 * gains].reshape(model_width),
        grad_up,
        grad_down,
    )


def solution(mesh):
    in_specs = (
        P("dp", None, None),
        P("dp", None),
        P("dp", None),
        P(),
        P("tensor", None),
        P("tensor", None),
        P("tensor"),
        P(),
        P(),
        P(),
        P(),
        P(None, "tensor"),
        P(None, "tensor"),
        P("tensor", None),
        P(),
        P(None, "tensor"),
        P("tensor", None),
        P("dp", "tensor", None),
    )
    out_specs = (
        P("dp", "tensor", None),
        P("dp", "tensor", None),
        P(),
        P(("tensor", "dp"), None),
        P(("tensor", "dp"), None),
        P(("tensor", "dp")),
        P(("tensor", "dp"), None),
        P(),
        P(),
        P(),
        P("dp", "tensor"),
        P("dp", "tensor"),
        P(("tensor", "dp"), None),
        P(),
        P("dp", "tensor"),
        P(("tensor", "dp"), None),
    )
    return jax.shard_map(
        functools.partial(on_device, dp=mesh.shape["dp"]),
        mesh=mesh,
        in_specs=in_specs,
        out_specs=out_specs,
        check_vma=False,
    )
```

```python
import functools

import jax
import jax.numpy as jnp
from jax import lax
from jax.experimental import pallas as pl
from jax.experimental.pallas import tpu as pltpu
from jax.sharding import PartitionSpec as P

epsilon = 1e-06
dims_rows = (((0,), (0,)), ((), ()))
dims_cols = (((1,), (1,)), ((), ()))
f32 = jnp.float32
bf16 = jnp.bfloat16

CHUNK = 64
UNROLL = 8


def cost(microseconds):
    return pl.CostEstimate(flops=0, bytes_accessed=int(1.7e6 * microseconds), transcendentals=0)


def rms_norm(values, gain):
    return values * lax.rsqrt(jnp.mean(values * values, axis=-1, keepdims=True) + epsilon) * gain


def silu(values):
    return values * jax.nn.sigmoid(values)


def silu_slope(values):
    sigma = jax.nn.sigmoid(values)
    return sigma * (1.0 + values * (1.0 - sigma))


def matmul(left, right):
    return jnp.dot(left, right, preferred_element_type=f32)


def inner_rows(left, right):
    return lax.dot_general(left, right, dims_rows, preferred_element_type=f32)


def inner_cols(left, right):
    return lax.dot_general(left, right, dims_cols, preferred_element_type=f32)


def store_part(part_ref, row, values):
    for lane_group in range(part_ref.shape[0]):
        part_ref[lane_group, pl.ds(pl.multiple_of(row * 8, 8), 8), :] = values[
            :, lane_group * 128 : (lane_group + 1) * 128
        ]


def sum_parts(part_ref):
    columns = []
    for lane_group in range(part_ref.shape[0]):
        total = part_ref[lane_group, pl.ds(0, CHUNK, stride=8), :]
        for sub in range(1, 8):
            total = total + part_ref[lane_group, pl.ds(sub, CHUNK, stride=8), :]
        columns.append(total)
    return jnp.concatenate(columns, axis=1)


def ema_forward_kernel(
    alive_ref, x_ref, keep_ref, blend_ref, skip_ref, mixed_ref, out_ref, tok_ref, part_ref
):
    states, width = keep_ref.shape
    length = x_ref.shape[0]
    keep = keep_ref[...]
    blend = blend_ref[...]
    half = states // 2
    tok_ref[0, 0] = 0.0

    def chunk(index, u):
        first = pl.multiple_of(index * CHUNK, CHUNK)

        def group(group_index, u):
            for step in range(UNROLL):
                row = group_index * UNROLL + step
                token = first + row
                u = (keep * alive_ref[token]) * u + x_ref[pl.ds(token, 1), :]
                term = u * blend
                store_part(part_ref, row, term[:half] + term[half:])
            return u

        u = lax.fori_loop(0, CHUNK // UNROLL, group, u)
        mixed = sum_parts(part_ref) + skip_ref[...] * x_ref[pl.ds(first, CHUNK), :]
        mixed_ref[pl.ds(first, CHUNK), :] = mixed
        out_ref[pl.ds(first, CHUNK), :] = silu(mixed).astype(bf16)
        return u

    lax.fori_loop(0, length // CHUNK, chunk, jnp.zeros((states, width), f32))


def ema_forward(alive, source, keep, blend, skip, group, hold, mixed=None):
    length = source.shape[0]
    states = keep.shape[0]
    channels = source.shape[1] // 2
    at = lambda rows: pl.BlockSpec((rows, channels), lambda i: (0, group))
    whole = pl.BlockSpec((length, channels), lambda i: (0, 0))
    smem = pl.BlockSpec(memory_space=pltpu.SMEM)
    count = 5
    hold = (() if mixed is None else (mixed,)) + tuple(hold)

    def body(*refs):
        ema_forward_kernel(*refs[:count], *refs[count + len(hold) :])

    return pl.pallas_call(
        body,
        grid=(1,),
        in_specs=[smem, at(length), at(states), at(states), at(1)]
        + [pl.BlockSpec(memory_space=pl.ANY)] * len(hold),
        out_specs=[at(length), whole, smem],
        out_shape=[
            jax.ShapeDtypeStruct((length, 2 * channels), f32),
            jax.ShapeDtypeStruct((length, channels), bf16),
            jax.ShapeDtypeStruct((1, 1), f32),
        ],
        scratch_shapes=[pltpu.VMEM((channels // 128, CHUNK * 8, 128), f32)],
        input_output_aliases={} if mixed is None else {count: 0},
        compiler_params=pltpu.CompilerParams(vmem_limit_bytes=12 << 20),
        cost_estimate=cost(6.3),
        name="ema_forward",
    )(alive, source, keep, blend, skip, *hold)


def ema_source_kernel(alive_ref, dm_ref, keep_ref, blend_ref, skip_ref, ds_ref, tok_ref, part_ref):
    states, width = keep_ref.shape
    length = dm_ref.shape[0]
    keep = keep_ref[...]
    blend = blend_ref[...]
    half = states // 2
    tok_ref[0, 0] = 0.0

    def chunk(index, v):
        back = pl.multiple_of(length - CHUNK - index * CHUNK, CHUNK)

        def group(group_index, v):
            for step in range(UNROLL):
                row = CHUNK - 1 - (group_index * UNROLL + step)
                token = back + row
                v = dm_ref[pl.ds(token, 1), :] + (keep * alive_ref[token + 1]) * v
                term = v * blend
                store_part(part_ref, row, term[:half] + term[half:])
            return v

        v = lax.fori_loop(0, CHUNK // UNROLL, group, v)
        ds_ref[pl.ds(back, CHUNK), :] = (
            sum_parts(part_ref) + skip_ref[...] * dm_ref[pl.ds(back, CHUNK), :]
        )
        return v

    lax.fori_loop(0, length // CHUNK, chunk, jnp.zeros((states, width), f32))


def ema_source(alive, d_mixed, keep, blend, skip, hold):
    length, channels = d_mixed.shape
    states = keep.shape[0]
    whole = lambda rows: pl.BlockSpec((rows, channels), lambda i: (0, 0))
    smem = pl.BlockSpec(memory_space=pltpu.SMEM)
    count = 5

    def body(*refs):
        ema_source_kernel(*refs[:count], *refs[count + len(hold) :])

    return pl.pallas_call(
        body,
        grid=(1,),
        in_specs=[smem, whole(length), whole(states), whole(states), whole(1)]
        + [pl.BlockSpec(memory_space=pl.ANY)] * len(hold),
        out_specs=[whole(length), smem],
        out_shape=[
            jax.ShapeDtypeStruct((length, channels), f32),
            jax.ShapeDtypeStruct((1, 1), f32),
        ],
        scratch_shapes=[pltpu.VMEM((channels // 128, CHUNK * 8, 128), f32)],
        compiler_params=pltpu.CompilerParams(vmem_limit_bytes=16 << 20),
        cost_estimate=cost(10.0),
        name="ema_source",
    )(alive, d_mixed, keep, blend, skip, *hold)


def ema_rates_kernel(alive_ref, x_ref, dm_ref, keep_ref, b_ref, g_ref, k_ref, tok_ref):
    states, width = keep_ref.shape
    length = x_ref.shape[0]
    keep = keep_ref[...]
    tok_ref[0, 0] = 0.0

    def group(group_index, carry):
        u, w, b_sum, g_sum = carry
        for step in range(UNROLL):
            token = group_index * UNROLL + step
            alive = alive_ref[token]
            dm = dm_ref[pl.ds(token, 1), :]
            kept = alive * u
            w = keep * (alive * w) + kept
            u = keep * kept + x_ref[pl.ds(token, 1), :]
            b_sum = b_sum + dm * u
            g_sum = g_sum + dm * w
        return u, w, b_sum, g_sum

    zero = jnp.zeros((states, width), f32)
    _, _, b_sum, g_sum = lax.fori_loop(0, length // UNROLL, group, (zero,) * 4)
    b_ref[...] = b_sum
    g_ref[...] = g_sum
    k_ref[...] = jnp.sum(x_ref[...] * dm_ref[...], axis=0, keepdims=True)


def ema_rates(alive, source, d_mixed, keep, hold):
    length, channels = source.shape
    states = keep.shape[0]
    width = min(256, channels)
    block = lambda rows: pl.BlockSpec((rows, width), lambda i: (0, i))
    smem = pl.BlockSpec(memory_space=pltpu.SMEM)
    count = 4

    def body(*refs):
        ema_rates_kernel(*refs[:count], *refs[count + len(hold) :])

    return pl.pallas_call(
        body,
        grid=(channels // width,),
        in_specs=[smem, block(length), block(length), block(states)]
        + [pl.BlockSpec(memory_space=pl.ANY)] * len(hold),
        out_specs=[block(states), block(states), block(1), smem],
        out_shape=[
            jax.ShapeDtypeStruct((states, channels), f32),
            jax.ShapeDtypeStruct((states, channels), f32),
            jax.ShapeDtypeStruct((1, channels), f32),
            jax.ShapeDtypeStruct((1, 1), f32),
        ],
        compiler_params=pltpu.CompilerParams(vmem_limit_bytes=16 << 20),
        cost_estimate=cost(14.0),
        name="ema_rates",
    )(alive, source, d_mixed, keep, *hold)


TILE = 256


def tile_call(kernel, steps, spot, ins, outs, scratch, microseconds, name, mib, hold=()):
    smem = pl.BlockSpec(memory_space=pltpu.SMEM)
    count = len(ins)

    def body(spot_ref, *refs):
        rest = refs[count + len(hold) :]
        rest[len(outs)][0, 0] = 0.0
        kernel(spot_ref, *refs[:count], *rest[: len(outs)], *rest[len(outs) + 1 :])

    return pl.pallas_call(
        body,
        grid_spec=pltpu.PrefetchScalarGridSpec(
            num_scalar_prefetch=1,
            grid=(steps,),
            in_specs=[
                pl.BlockSpec(block, index, pipeline_mode=pl.Buffered(1))
                if block == v.shape
                else pl.BlockSpec(block, index)
                for v, block, index in ins
            ]
            + [pl.BlockSpec(memory_space=pl.ANY)] * len(hold),
            out_specs=[pl.BlockSpec(block, index) for _, _, block, index in outs] + [smem],
            scratch_shapes=scratch,
        ),
        out_shape=[jax.ShapeDtypeStruct(shape, dtype) for shape, dtype, _, _ in outs]
        + [jax.ShapeDtypeStruct((1, 1), f32)],
        compiler_params=pltpu.CompilerParams(vmem_limit_bytes=mib << 20),
        cost_estimate=cost(microseconds),
        name=name,
    )(spot, *[v for v, _, _ in ins], *hold)


def whole_map(rank):
    return lambda i, s: (0,) * rank


def row_map(i, s):
    return (i, 0)


def slot_map(i, s):
    return (i // 2, 0, 0)


def norm_factor(values):
    return lax.rsqrt(jnp.mean(values * values, axis=-1, keepdims=True) + epsilon)


def by_core(c, groups):
    first = c == 0
    g0, g1, g2, g3 = groups
    mine = jnp.concatenate([jnp.where(first, g0, g1), jnp.where(first, g2, g3)], axis=1)
    theirs = jnp.concatenate([jnp.where(first, g1, g0), jnp.where(first, g3, g2)], axis=1)
    return mine, theirs


def lane_groups(values):
    width = values.shape[1] // 4
    return [values[:, k * width : (k + 1) * width] for k in range(4)]


def first_norm_kernel(spot, in_ref, gain_ref, normed_ref, source_ref, rows_ref):
    low = in_ref[0]
    values = low.astype(f32)

    @pl.when(lax.rem(pl.program_id(0), 2) == spot[1])
    def _():
        rows_ref[0] = low

    normed = (values * norm_factor(values) * gain_ref[...]).astype(bf16)
    normed_ref[...] = normed
    mine, _ = by_core(spot[1], lane_groups(normed.astype(f32)))
    rows = pl.program_id(0) * TILE + lax.broadcasted_iota(jnp.int32, mine.shape, 0)
    source_ref[...] = jnp.where(rows < spot[2], mine, 0.0)


def first_norm(spot, block_input, gain):
    _, length, width = block_input.shape
    return tile_call(
        first_norm_kernel,
        length // TILE,
        spot,
        [
            (block_input, (1, TILE, width), lambda i, s: (s[0], i, 0)),
            (gain[None], (1, width), whole_map(2)),
        ],
        [
            ((length, width), bf16, (TILE, width), row_map),
            ((length, width // 2), f32, (TILE, width // 2), row_map),
            ((2, TILE, width), bf16, (1, TILE, width), slot_map),
        ],
        [],
        2.5,
        "first_norm",
        12,
    )


def masked_scores(q, key, seg_rows, seg_cols, first_row):
    scores = inner_cols(q, key) * (q.shape[1] ** (-0.5))
    rows = first_row + lax.broadcasted_iota(jnp.int32, scores.shape, 0)
    cols = lax.broadcasted_iota(jnp.int32, scores.shape, 1)
    return jnp.where((seg_rows == seg_cols) | (rows == cols), scores, -1000000000.0)


def attend_kernel(
    spot, q_ref, k_ref, segr_ref, segc_ref, va_ref, vb_ref, ra_ref, rb_ref,
    attn_ref, heard_ref, lse_ref,
):
    step = pl.program_id(0)
    scores = masked_scores(q_ref[...], k_ref[...], segr_ref[...], segc_ref[...], step * TILE)
    top = jnp.max(scores, axis=1, keepdims=True)
    grown = jnp.exp(scores - top)
    total = jnp.sum(grown, axis=1, keepdims=True)
    prob = (grown * (1.0 / total)).astype(bf16)
    lse_ref[...] = top + jnp.log(total)
    cols = va_ref.shape[1]
    for side, (v_ref, r_ref) in enumerate(((va_ref, ra_ref), (vb_ref, rb_ref))):
        here = slice(side * cols, (side + 1) * cols)
        attn = matmul(prob, v_ref[...])
        attn_ref[:, here] = attn.astype(bf16)
        heard_ref[:, here] = (attn * silu(r_ref[...].astype(f32))).astype(bf16)


def attend(spot, query, key, seg_rows, seg_cols, values, resets):
    length, zdim = query.shape
    cols = values[0].shape[1]
    tile = lambda v: (v, (TILE, v.shape[1]), row_map)
    whole = lambda v: (v, v.shape, whole_map(2))
    out = ((length, 2 * cols), bf16, (TILE, 2 * cols), row_map)
    return tile_call(
        attend_kernel,
        length // TILE,
        spot,
        [tile(query), whole(key), tile(seg_rows), whole(seg_cols)]
        + [whole(v) for v in values]
        + [tile(r) for r in resets],
        [out] * 2 + [((length, 1), f32, (TILE, 1), row_map)],
        [],
        6.2,
        "attend",
        24,
    )


def out_kernel(spot, heard_ref, wa_ref, wb_ref, mine_ref, theirs_ref):
    depth = wa_ref.shape[0]
    result = matmul(heard_ref[:, :depth], wa_ref[...]) + matmul(heard_ref[:, depth:], wb_ref[...])
    is_mine = lax.rem(pl.program_id(0), 2) == spot[1]

    @pl.when(is_mine)
    def _():
        mine_ref[0] = result.astype(bf16)

    @pl.when(jnp.logical_not(is_mine))
    def _():
        theirs_ref[0] = result.astype(bf16)


def out_rows(spot, heard, weights):
    length, depth = heard.shape
    width = weights[0].shape[1]
    side = ((2, TILE, width), bf16, (1, TILE, width), slot_map)
    return tile_call(
        out_kernel,
        length // TILE,
        spot,
        [(heard, (TILE, depth), row_map)] + [(w, w.shape, whole_map(2)) for w in weights],
        [side, side],
        [],
        4.5,
        "out_rows",
        16,
    )


def attend_back_kernel(
    spot, dm_ref, q_ref, k_ref, segr_ref, segc_ref, lse_ref, a_ref,
    woa_ref, wob_ref, va_ref, vb_ref, pva_ref, pvb_ref, wra_ref, wrb_ref, pra_ref, prb_ref,
    dpr_ref, dpv_ref, dq_ref, dk_ref, mine_ref, theirs_ref,
    dva_ref, dvb_ref,
):
    step = pl.program_id(0)
    cols = va_ref.shape[1]
    scale = q_ref.shape[1] ** (-0.5)
    scores = masked_scores(q_ref[...], k_ref[...], segr_ref[...], segc_ref[...], step * TILE)
    prob = jnp.exp(scores - lse_ref[...])
    prob_low = prob.astype(bf16)
    d_middle = dm_ref[...]
    d_prob = None
    d_ema = None

    @pl.when(step == 0)
    def _():
        dk_ref[...] = jnp.zeros_like(dk_ref)
        dva_ref[...] = jnp.zeros_like(dva_ref)
        dvb_ref[...] = jnp.zeros_like(dvb_ref)

    for side, (wo_ref, v_ref, wr_ref, pr_ref, dv_ref) in enumerate(
        ((woa_ref, va_ref, wra_ref, pra_ref, dva_ref), (wob_ref, vb_ref, wrb_ref, prb_ref, dvb_ref))
    ):
        here = slice(side * cols, (side + 1) * cols)
        d_heard = inner_cols(d_middle, wo_ref[...])
        pre = pr_ref[...].astype(f32)
        sigma = jax.nn.sigmoid(pre)
        d_attn = (d_heard * (pre * sigma)).astype(bf16)
        slope = sigma * (1.0 + pre * (1.0 - sigma))
        d_reset = (d_heard * a_ref[:, here].astype(f32) * slope).astype(bf16)
        dpr_ref[:, here] = d_reset
        part = inner_cols(d_attn, v_ref[...])
        d_prob = part if d_prob is None else d_prob + part
        dv_ref[...] += inner_rows(prob_low, d_attn)
        part = inner_cols(d_reset, wr_ref[...])
        d_ema = part if d_ema is None else d_ema + part
    mine, theirs = by_core(spot[1], lane_groups(d_ema))
    mine_ref[...] = mine
    theirs_ref[...] = theirs.astype(bf16)
    inner = jnp.sum(prob * d_prob, axis=1, keepdims=True)
    d_scores = (prob * (d_prob - inner)).astype(bf16)
    dq_ref[...] = matmul(d_scores, k_ref[...]) * scale
    dk_ref[...] += inner_rows(d_scores, q_ref[...]) * scale

    @pl.when(step == pl.num_programs(0) - 1)
    def _():
        for side, (pv_ref, dv_ref) in enumerate(((pva_ref, dva_ref), (pvb_ref, dvb_ref))):
            here = slice(side * cols, (side + 1) * cols)
            dpv_ref[:, here] = (dv_ref[...] * silu_slope(pv_ref[...].astype(f32))).astype(bf16)


def attend_back(hold, spot, d_middle, query, key, seg_rows, seg_cols, lse, attn, outs, values, pre_values, w_resets, pre_resets):
    length, zdim = query.shape
    cols = values[0].shape[1]
    width = outs[0].shape[1]
    tile = lambda v: (v, (TILE, v.shape[1]), row_map)
    whole = lambda v: (v, v.shape, whole_map(2))
    return tile_call(
        attend_back_kernel,
        length // TILE,
        spot,
        [tile(d_middle), tile(query), whole(key), tile(seg_rows), whole(seg_cols), tile(lse), tile(attn)]
        + [whole(v) for v in outs + values + pre_values + w_resets]
        + [tile(v) for v in pre_resets],
        [
            ((length, 2 * cols), bf16, (TILE, 2 * cols), row_map),
            ((length, 2 * cols), bf16, (length, 2 * cols), whole_map(2)),
            ((length, zdim), f32, (TILE, zdim), row_map),
            ((length, zdim), f32, (length, zdim), whole_map(2)),
            ((length, width // 2), f32, (TILE, width // 2), row_map),
            ((length, width // 2), bf16, (TILE, width // 2), row_map),
        ],
        [pltpu.VMEM((length, cols), f32)] * 2,
        21.0,
        "attend_back",
        36,
        hold,
    )


def second_norm_kernel(
    spot, in_ref, part_ref, got_ref, gain_ref, middle_ref, normed_ref, one_ref, two_ref
):
    middle = in_ref[0].astype(f32) + part_ref[0].astype(f32) + got_ref[0].astype(f32)
    middle_ref[0] = middle
    normed = (middle * norm_factor(middle) * gain_ref[...]).astype(bf16)
    normed_ref[0] = normed

    @pl.when(pl.program_id(0) == 0)
    def _():
        one_ref[...] = normed

    @pl.when(pl.program_id(0) > 0)
    def _():
        two_ref[...] = normed


def second_norm(spot, in_rows, part, got, gain, hold):
    slots, quarter, width = part.shape
    slot = lambda v: (v, (1, quarter, width), lambda i, s: (i, 0, 0))
    single = ((quarter, width), bf16, (quarter, width), whole_map(2))
    return tile_call(
        second_norm_kernel,
        slots,
        spot,
        [
            slot(in_rows),
            slot(part),
            slot(got),
            (gain[None], (1, width), whole_map(2)),
        ],
        [
            ((slots, quarter, width), f32, (1, quarter, width), lambda i, s: (i, 0, 0)),
            ((slots, quarter, width), bf16, (1, quarter, width), lambda i, s: (i, 0, 0)),
            single,
            single,
        ],
        [],
        3.0,
        "second_norm",
        16,
        hold,
    )


def chip_sum(spot, both, got):
    rows, width = got.shape

    def kernel(s, near_ref, got_ref, out_ref):
        out_ref[...] = (near_ref[...].astype(f32) + got_ref[...].astype(f32)).astype(bf16)

    return tile_call(
        kernel,
        1,
        spot,
        [(both, (rows, width), whole_map(2)), (got, got.shape, whole_map(2))],
        [((rows, width), bf16, (rows, width), whole_map(2))],
        [],
        1.5,
        "chip_sum",
        8,
    )


def second_norm_back_kernel(
    spot, near_ref, got_ref, far_ref, middle_ref, cot_ref, gain_ref, dm_ref, low_ref, gain_out_ref
):
    grad = near_ref[0].astype(f32) + got_ref[0].astype(f32) + far_ref[...].astype(f32)
    middle = middle_ref[0]
    factor = norm_factor(middle)
    scaled = grad * gain_ref[...]
    shift = jnp.mean(middle * scaled, axis=-1, keepdims=True) * (factor * factor * factor)
    d_middle = cot_ref[0, 0].astype(f32) + factor * scaled - middle * shift
    dm_ref[...] = d_middle
    low_ref[...] = d_middle.astype(bf16)
    part = jnp.sum(grad * middle * factor, axis=0, keepdims=True)

    @pl.when(pl.program_id(0) == 0)
    def _():
        gain_out_ref[...] = part

    @pl.when(pl.program_id(0) > 0)
    def _():
        gain_out_ref[...] += part


def second_norm_back(spot, slot, near, got, far, middle, cot, gain):
    _, quarter, width = middle.shape
    tile = quarter // 2
    pair = lambda v: (v, (1, tile, width), lambda i, s: (slot, i, 0))
    out = lambda dtype: ((quarter, width), dtype, (tile, width), row_map)
    return tile_call(
        second_norm_back_kernel,
        2,
        spot,
        [
            pair(near),
            pair(got),
            (far, (tile, width), row_map),
            pair(middle),
            (cot, (1, 1, tile, width), lambda i, s: (s[0], slot, i, 0)),
            (gain[None], (1, width), whole_map(2)),
        ],
        [out(f32), out(bf16), ((1, width), f32, (1, width), whole_map(2))],
        [],
        3.0,
        "second_norm_back",
        12,
    )


def first_norm_back_kernel(
    spot, in_ref, part_ref, got_ref, src_ref, far_ref, dm0_ref, dm1_ref, gain_ref, grad_ref,
    gain_out_ref,
):
    step = pl.program_id(0)
    quarter, half = src_ref.shape[1:]
    first = spot[1] == 0
    near = src_ref[0]
    far = far_ref[0].astype(f32)
    groups = []
    for k in range(2):
        own = near[:, k * half // 2 : (k + 1) * half // 2]
        other = far[:, k * half // 2 : (k + 1) * half // 2]
        groups += [jnp.where(first, own, other), jnp.where(first, other, own)]
    source = jnp.concatenate(groups, axis=1)
    rows = (spot[1] + 2 * step) * quarter + lax.broadcasted_iota(jnp.int32, source.shape, 0)
    source = jnp.where(rows < spot[2], source, 0.0)
    grad = part_ref[0].astype(f32) + got_ref[0].astype(f32) + source
    values = in_ref[0].astype(f32)
    factor = norm_factor(values)
    scaled = grad * gain_ref[...]
    shift = jnp.mean(values * scaled, axis=-1, keepdims=True) * (factor * factor * factor)
    d_middle = jnp.where(step == 0, dm0_ref[...], dm1_ref[...])
    grad_ref[0] = (d_middle + factor * scaled - values * shift).astype(bf16)
    part = jnp.sum(grad * values * factor, axis=0, keepdims=True)

    @pl.when(step == 0)
    def _():
        gain_out_ref[...] = part

    @pl.when(step > 0)
    def _():
        gain_out_ref[...] += part


def first_norm_back(spot, in_rows, part, got, source, source_far, d_middle, gain, hold):
    slots = 2
    quarter, width = d_middle[0].shape
    mine = lambda v: (
        v.reshape(4, quarter, v.shape[1]),
        (1, quarter, v.shape[1]),
        lambda i, s: (s[1] + 2 * i, 0, 0),
    )
    slot = lambda v, w: (v.reshape(slots, quarter, w), (1, quarter, w), lambda i, s: (i, 0, 0))
    return tile_call(
        first_norm_back_kernel,
        slots,
        spot,
        [
            slot(in_rows, width),
            mine(part),
            slot(got, width),
            mine(source),
            slot(source_far, width // 2),
            (d_middle[0], (quarter, width), whole_map(2)),
            (d_middle[1], (quarter, width), whole_map(2)),
            (gain[None], (1, width), whole_map(2)),
        ],
        [
            ((slots, quarter, width), bf16, (1, quarter, width), lambda i, s: (i, 0, 0)),
            ((1, width), f32, (1, width), whole_map(2)),
        ],
        [],
        3.0,
        "first_norm_back",
        20,
        hold,
    )


def core_swap(values):
    return lax.ppermute(values, "tensor", [(0, 1), (1, 0), (2, 3), (3, 2)])


def y_swap(values):
    return lax.ppermute(values, "tensor", [(0, 2), (2, 0), (1, 3), (3, 1)])


def dp_swap(values, dp, mask):
    return lax.ppermute(values, "dp", [(i, i ^ mask) for i in range(dp)])


def pick(values, index, axis=0):
    return lax.dynamic_index_in_dim(values, index, axis, keepdims=False)


def ordered(flag, first, second, axis):
    return jnp.concatenate(
        [jnp.where(flag, first, second), jnp.where(flag, second, first)], axis=axis
    )


def whole_in(v):
    return (v, v.shape, whole_map(v.ndim))


def whole_out(shape, dtype):
    return (shape, dtype, shape, whole_map(len(shape)))


def rows_at(number, rows):
    return pl.ds(pl.multiple_of(number * rows, rows), rows)


def add_low(left, right):
    return (left.astype(f32) + right.astype(f32)).astype(bf16)


def send_first(spot, g_reset, g_value, dp):
    line = dp // 2
    rows = g_reset.shape[0] // dp
    cols = g_reset.shape[1] // 2

    def kernel(s, reset_ref, value_ref, reset_out, value_out):
        x = lax.rem(s[3], 2)
        for h in range(line):
            at = rows_at(2 * h + 1 - x, rows)
            reset_out[0, h] = reset_ref[at, :cols]
            reset_out[1, h] = reset_ref[at, cols:]
        value_out[...] = value_ref[:, cols:]

    reset_sent, value_sent, _ = tile_call(
        kernel,
        1,
        spot,
        [whole_in(g_reset), whole_in(g_value)],
        [
            whole_out((2, line, rows, cols), bf16),
            whole_out((g_value.shape[0], cols), bf16),
        ],
        [],
        2.5,
        "send_first",
        14,
    )
    return reset_sent, value_sent


def out_first(spot, g_out, dp):
    line = dp // 2
    rows = g_out.shape[0] // (2 * dp)
    width = g_out.shape[1]

    def kernel(s, in_ref, out_ref):
        x = lax.rem(s[3], 2)
        for side in range(2):
            for h in range(line):
                out_ref[side, h] = in_ref[rows_at(side * dp + 2 * h + 1 - x, rows), :]

    out = whole_out((2, line, rows, width), bf16)
    return tile_call(kernel, 1, spot, [whole_in(g_out)], [out], [], 1.7, "out_first", 10)[0]


def out_second(spot, g_out, got, dp, hold):
    line = dp // 2
    rows = g_out.shape[0] // (2 * dp)
    width = g_out.shape[1]

    def kernel(s, near_ref, got_ref, sent_ref, kept_ref):
        x = lax.rem(s[3], 2)
        for h in range(line):
            kept_ref[h] = add_low(near_ref[rows_at(2 * h + x, rows), :], got_ref[0, h])
            sent_ref[h] = add_low(near_ref[rows_at(dp + 2 * h + x, rows), :], got_ref[1, h])

    out = whole_out((line, rows, width), bf16)
    sent, kept, _ = tile_call(
        kernel,
        1,
        spot,
        [whole_in(g_out), whole_in(got)],
        [out, out],
        [],
        2.5,
        "out_second",
        12,
        hold,
    )
    return sent, kept


def second_stage(spot, g_reset, reset_got, g_value, value_got, dp, hold):
    line = dp // 2
    rows = g_reset.shape[0] // dp
    cols = g_reset.shape[1] // 2

    def kernel(s, reset_ref, rgot_ref, value_ref, vgot_ref, rsent_ref, rkept_ref, vsent_ref, vkept_ref):
        x = lax.rem(s[3], 2)
        for h in range(line):
            here = rows_at(2 * h + x, rows)
            there = rows_at(2 * h + 1 - x, rows)
            rkept_ref[h] = add_low(reset_ref[here, :cols], rgot_ref[0, h])
            rsent_ref[h] = add_low(reset_ref[here, cols:], rgot_ref[1, h])
            vkept_ref[h] = add_low(value_ref[here, :cols], vgot_ref[here, :])
            vsent_ref[h] = add_low(value_ref[there, :cols], vgot_ref[there, :])

    out = whole_out((line, rows, cols), bf16)
    return tile_call(
        kernel,
        1,
        spot,
        [whole_in(v) for v in (g_reset, reset_got, g_value, value_got)],
        [out] * 4,
        [],
        4.0,
        "second_stage",
        20,
        hold,
    )


def merge_stage(spot, pairs, hold):
    (out_kept, _), (reset_kept, _), _ = pairs
    line, rows, cols = reset_kept.shape
    total_rows = rows + out_kept.shape[1]
    width = out_kept.shape[2]

    def kernel(s, ok, og, rk, rg, vk, vg, sent_ref, kept_ref):
        bit = lax.rem(lax.div(s[3], 2), 2)
        for q in range(line // 2):
            for side, out_ref in ((1 - bit, sent_ref), (bit, kept_ref)):
                h = 2 * q + side
                out_ref[q, :rows, :cols] = add_low(rk[h], rg[h])
                out_ref[q, :rows, cols:] = add_low(vk[h], vg[h])
                out_ref[q, rows:, :] = add_low(ok[h], og[h])

    out = whole_out((line // 2, total_rows, width), bf16)
    sent, kept, tok = tile_call(
        kernel,
        1,
        spot,
        [whole_in(v) for pair in pairs for v in pair],
        [out, out],
        [],
        4.0,
        "merge_stage",
        20,
        hold,
    )
    return sent, kept, tok


def line_stage(spot, kept, got, bit, hold):
    count, rows, width = kept.shape

    def kernel(s, kept_ref, got_ref, sent_ref, out_ref):
        side_here = lax.rem(lax.div(s[3], 1 << bit), 2)
        for q in range(count // 2):
            for side, ref in ((1 - side_here, sent_ref), (side_here, out_ref)):
                ref[q] = add_low(kept_ref[2 * q + side], got_ref[2 * q + side])

    out = whole_out((count // 2, rows, width), bf16)
    sent, kept, tok = tile_call(
        kernel, 1, spot, [whole_in(kept), whole_in(got)], [out, out], [], 3.0, "line_stage", 12, hold
    )
    return sent, kept, tok


def last_stage(spot, kept, got, rows, cols):
    def kernel(s, kept_ref, got_ref, out_ref, reset_ref, value_ref):
        total = lambda at, to: kept_ref[0, at, to].astype(f32) + got_ref[0, at, to].astype(f32)
        first = slice(0, rows)
        reset_ref[...] = total(first, slice(0, cols))
        value_ref[...] = total(first, slice(cols, 2 * cols))
        out_ref[...] = total(slice(rows, kept_ref.shape[1]), slice(None))

    part = whole_out((rows, cols), f32)
    return tile_call(
        kernel,
        1,
        spot,
        [whole_in(kept), whole_in(got)],
        [whole_out((kept.shape[1] - rows, kept.shape[2]), f32), part, part],
        [],
        2.0,
        "last_stage",
        8,
    )[:3]


def pack_kernel(
    spot, norm_ref, gain0_ref, gain1_ref, dq_ref, dk_ref, shared_ref, b_ref, g_ref, skip_ref,
    mix_ref, forget_ref, out_ref,
):
    width = out_ref.shape[2]
    leader = (1 - spot[1]).astype(f32)
    shared = shared_ref[...]
    total = lambda v: jnp.sum(v, axis=0, keepdims=True)
    query = jnp.concatenate([total(dq_ref[...] * shared), total(dq_ref[...])], axis=1) * leader
    key = jnp.concatenate([total(dk_ref[...] * shared)] * 2, axis=1) * leader
    gain = gain0_ref[...] + gain1_ref[...]
    parts = norm_ref.shape[1] // width
    forget = mix_ref[...] * (b_ref[...] - forget_ref[...] * g_ref[...])
    mix = forget_ref[...] * b_ref[...]
    states = forget.shape[0]
    head = out_ref.shape[1] - 2 * states
    for target in range(4):
        out_ref[target, :head, :] = jnp.zeros((head, width), f32)
        for part in range(parts):
            here = slice(part * width, (part + 1) * width)
            out_ref[target, part : part + 1, :] = norm_ref[:, here]
            out_ref[target, parts + part : parts + part + 1, :] = gain[:, here]
        out_ref[target, 2 * parts : 2 * parts + 1, :] = query
        out_ref[target, 2 * parts + 1 : 2 * parts + 2, :] = key
        here = slice((target // 2) * width, (target // 2 + 1) * width)
        mine = (spot[1] == target % 2).astype(f32)
        out_ref[target, 2 * parts + 2 : 2 * parts + 3, :] = skip_ref[:, here] * mine
        out_ref[target, head : head + states, :] = forget[:, here] * mine
        out_ref[target, head + states :, :] = mix[:, here] * mine


def pack(spot, arrays, states, channels, hold):
    head = 16
    return tile_call(
        pack_kernel,
        1,
        spot,
        [whole_in(v) for v in arrays],
        [whole_out((4, head + 2 * states, channels), f32)],
        [],
        3.0,
        "pack",
        10,
        hold,
    )[0]


def on_device(
    block_input,
    segment_ids,
    pad_mask,
    norm_gain,
    ema_forget,
    ema_mix,
    ema_skip,
    proj_shared,
    query_gain,
    query_bias,
    key_gain,
    proj_value,
    proj_reset,
    proj_out,
    ffn_gain,
    ffn_up,
    ffn_down,
    cotangent,
    *,
    dp,
):
    shard = lax.axis_index("tensor")
    place = lax.axis_index("dp")
    y = shard // 2
    c = shard % 2
    is_first_y = y == 0
    is_first_c = c == 0
    length, model_width = block_input.shape[1:]
    zdim = proj_shared.shape[1]
    channels, states = ema_forget.shape
    quarter = cotangent.shape[1]

    def fetch(weight, after=None):
        halves = weight.reshape((2, weight.shape[0] // 2) + weight.shape[1:])
        half = pick(halves, place % 2)
        if after is not None:
            half = half + after[:1, :1] * 0
        direct = y_swap(half)
        around = dp_swap(direct, dp, 1)
        return ordered(place % 2 == 0, direct, around, 0), direct, around

    def their_rows(values):
        return pick(values.reshape(2, 2, quarter, values.shape[1]), 1 - c, 1)

    def my_channels(values):
        split = values.reshape(2, 2, channels, values.shape[1])
        return pick(split, c, 1).reshape(2 * channels, values.shape[1])

    own_params = jnp.concatenate([ema_forget.T, ema_mix.T, ema_skip[None]], axis=0)
    params = ordered(is_first_y, own_params, y_swap(own_params), 1)
    forget = params[:states]
    mix = params[states : 2 * states]
    skip = params[2 * states :]
    keep = 1.0 - forget
    blend = forget * mix

    value_far, direct_value, _ = fetch(proj_value)
    reset_far, direct_reset, around_reset = fetch(proj_reset, direct_value)
    out_far, direct_out, _ = fetch(proj_out, direct_reset)
    cotangent = cotangent + (direct_out[0, 0] * 0).astype(bf16)
    cot_far = y_swap(cotangent)

    segments = pick(segment_ids, y)
    padding = pick(pad_mask, y)
    spot = jnp.stack([y, c, jnp.sum(padding), place]).astype(jnp.int32)
    alive = jnp.concatenate(
        [jnp.zeros((1,), f32), (segments[1:] == segments[:-1]).astype(f32), jnp.zeros((1,), f32)]
    )
    seg_rows = segments[:, None]
    seg_cols = jnp.where(padding > 0, segments, -1)[None]

    normed, source, in_rows, _ = first_norm(spot, block_input, norm_gain)
    mixed, ema_0, _ = ema_forward(alive, source, keep, blend, skip, 0, ())
    mixed, ema_1, _ = ema_forward(alive, source, keep, blend, skip, 1, (direct_value,), mixed)
    got_0 = core_swap(ema_0)
    got_1 = core_swap(ema_1)
    ema_all = jnp.concatenate(
        [
            jnp.where(is_first_c, ema_0, got_0),
            jnp.where(is_first_c, got_0, ema_0),
            jnp.where(is_first_c, ema_1, got_1),
            jnp.where(is_first_c, got_1, ema_1),
        ],
        axis=1,
    )

    pre_shared = matmul(ema_all, proj_shared) + around_reset[:1, :1].astype(f32) * 0.0
    shared = silu(pre_shared)
    query = (shared * query_gain + query_bias).astype(bf16)
    key = (shared * key_gain).astype(bf16)
    pre_values = [matmul(normed, w).astype(bf16) for w in (proj_value, value_far)]
    values = [silu(v.astype(f32)).astype(bf16) for v in pre_values]
    pre_resets = [matmul(ema_all, w).astype(bf16) for w in (proj_reset, reset_far)]
    attn, heard, lse, _ = attend(spot, query, key, seg_rows, seg_cols, values, pre_resets)
    out_mine, out_theirs, _ = out_rows(spot, heard, [proj_out, out_far])
    middle, normed_two, normed_0, normed_1, _ = second_norm(
        spot, in_rows, out_mine, core_swap(out_theirs), ffn_gain, (cot_far,)
    )

    cot_mine = ordered(is_first_y, cotangent[:, None], cot_far[:, None], 1)
    cot_theirs = core_swap(cot_mine)

    far_0 = y_swap(normed_0)
    far_1 = y_swap(normed_1)
    rows = lambda v: v.reshape(-1, model_width)

    def piece(two, cot):
        d_hidden = inner_cols(cot, ffn_down).astype(bf16)
        pre_up = matmul(two, ffn_up)
        hidden = silu(pre_up).astype(bf16)
        d_pre = (d_hidden.astype(f32) * silu_slope(pre_up)).astype(bf16)
        d_two = inner_cols(d_pre, ffn_up).astype(bf16)
        result = matmul(hidden, ffn_down).astype(bf16)
        return two, cot, hidden, d_pre, d_two, result

    def far_piece(far, slot, after):
        far = far + (after[0, 0] * 0).astype(bf16)
        two = jnp.concatenate([far, core_swap(far)], axis=0)
        cot = jnp.concatenate(
            [pick(cot_mine, 1 - y)[slot], pick(cot_theirs, 1 - y)[slot]], axis=0
        )
        return piece(two, cot)

    own = piece(
        jnp.concatenate([rows(normed_two), rows(core_swap(normed_two))], axis=0),
        jnp.concatenate([rows(pick(cot_mine, y)), rows(pick(cot_theirs, y))], axis=0),
    )
    far_p0 = far_piece(far_0, 0, own[4])
    far_p1 = far_piece(far_1, 1, far_p0[4])
    pieces = [own, far_p0, far_p1]

    def place_rows(rows):
        arrived = y_swap(pick(rows, 1 - y))
        return ordered(is_first_y, pick(rows, y)[None], arrived[None], 0)

    slots = lambda v: v.reshape(2, quarter, model_width)
    sum_f0, _ = chip_sum(spot, far_p0[4], core_swap(far_p0[4][quarter:]))
    sum_f1, tok_two = chip_sum(spot, far_p1[4], core_swap(far_p1[4][quarter:]))
    d_two_f0 = y_swap(sum_f0)
    d_two_f1 = y_swap(sum_f1)
    d_two_own = slots(own[4][: 2 * quarter])
    d_two_got = slots(core_swap(own[4][2 * quarter :]))
    d_mid_0, low_0, gain_0, _ = second_norm_back(
        spot, 0, d_two_own, d_two_got, d_two_f0, middle, cot_mine, ffn_gain
    )
    d_mid_1, low_1, gain_1, tok_mid = second_norm_back(
        spot, 1, d_two_own, d_two_got, d_two_f1, middle, cot_mine, ffn_gain
    )
    g_down = sum(inner_rows(hidden, cot) for _, cot, hidden, _, _, _ in pieces)
    g_down = (g_down + tok_two[0, 0]).astype(bf16)
    g_up = sum(inner_rows(two, d_pre) for two, _, _, d_pre, _, _ in pieces)
    g_up = (g_up + tok_two[0, 0]).astype(bf16)
    ffn_shares = jnp.concatenate(
        [v.reshape(dp, v.shape[0] // dp, v.shape[1]) for v in (g_down, g_up)], axis=1
    )
    grad_ffn = lax.psum_scatter(ffn_shares, "dp", scatter_dimension=0, tiled=True)[0].astype(f32)
    grad_down = grad_ffn[: g_down.shape[0] // dp]
    grad_up = grad_ffn[g_down.shape[0] // dp :]
    got_0 = core_swap(low_0)
    got_1 = core_swap(low_1)
    d_middle = jnp.concatenate(
        [
            jnp.where(is_first_c, low_0, got_0),
            jnp.where(is_first_c, got_0, low_0),
            jnp.where(is_first_c, low_1, got_1),
            jnp.where(is_first_c, got_1, low_1),
        ],
        axis=0,
    )
    own_cols = proj_value.shape[1]
    g_out = inner_rows(heard, d_middle).astype(bf16)
    out_sent = out_first(spot, g_out, dp)
    out_got = dp_swap(out_sent, dp, 1)
    near_res, _ = chip_sum(spot, own[5], core_swap(own[5][2 * quarter :]))
    d_reset, d_value, d_query, d_key, d_ema_mine, d_ema_theirs, tok_back = attend_back(
        (out_sent, ffn_shares, near_res),
        spot,
        d_middle,
        query,
        key,
        seg_rows,
        seg_cols,
        lse,
        attn,
        [proj_out, out_far],
        values,
        pre_values,
        [proj_reset, reset_far],
        pre_resets,
    )
    far_res = jnp.stack([slots(far_p0[5]), slots(far_p1[5])], axis=1)
    far_res = far_res[0].astype(f32) + (core_swap(far_res[1]).astype(f32) + tok_mid[0, 0])
    far_res = y_swap(far_res.astype(bf16))
    res_rows = (
        slots(near_res).astype(f32)
        + far_res.astype(f32)
        + tok_back[0, 0]
    )
    block_output = place_rows((middle + res_rows).astype(bf16))

    g_reset = inner_rows(ema_all, d_reset).astype(bf16)
    g_value = inner_rows(normed, d_value).astype(bf16)
    reset_sent, value_sent = send_first(spot, g_reset, g_value, dp)
    reset_got = dp_swap(reset_sent, dp, 1)
    value_got = y_swap(value_sent)

    d_query_key = jnp.concatenate([d_query, d_key], axis=1)
    d_query_key = d_query_key + core_swap(d_query_key.astype(bf16)).astype(f32)
    d_query = d_query_key[:, :zdim]
    d_key = d_query_key[:, zdim:]
    d_shared = d_query * query_gain + d_key * key_gain
    d_pre_shared = (d_shared * silu_slope(pre_shared)).astype(bf16)
    g_shared = jnp.stack([inner_rows(ema_0, d_pre_shared), inner_rows(ema_1, d_pre_shared)])
    g_shared = pick(g_shared, y) + y_swap(pick(g_shared, 1 - y).astype(bf16)).astype(f32)
    d_ema = (
        inner_cols(d_pre_shared, my_channels(proj_shared))
        + d_ema_mine
        + core_swap(d_ema_theirs).astype(f32)
    )
    d_mixed = d_ema * silu_slope(mixed)
    d_source, tok_source = ema_source(
        alive, d_mixed, keep, blend, skip, (reset_sent, value_sent)
    )
    out_sent, out_kept = out_second(spot, g_out, out_got, dp, (tok_source,))
    out_got = y_swap(out_sent)
    b_sum, g_sum, g_skip, tok_rates = ema_rates(alive, source, d_mixed, keep, (out_sent,))
    reset_sent, reset_kept, value_sent, value_kept, _ = second_stage(
        spot, g_reset, reset_got, g_value, value_got, dp, (tok_rates,)
    )
    reset_got = y_swap(reset_sent)
    value_got = dp_swap(value_sent, dp, 1)
    d_normed = (
        inner_cols(d_value[:, :own_cols], proj_value) + inner_cols(d_value[:, own_cols:], value_far)
        + tok_rates[0, 0]
    ).astype(bf16)
    d_normed_got = core_swap(their_rows(d_normed))
    grad_rows, g_norm_gain, tok_rows = first_norm_back(
        spot,
        in_rows,
        d_normed,
        d_normed_got,
        d_source,
        core_swap((their_rows(d_source) + tok_rates[0, 0]).astype(bf16)),
        [d_mid_0, d_mid_1],
        norm_gain,
        (reset_sent, value_sent),
    )
    grad_input = place_rows(grad_rows)

    packed = pack(
        spot,
        (
            g_norm_gain, gain_0, gain_1, d_query, d_key, shared,
            b_sum, g_sum, g_skip, mix, forget,
        ),
        states,
        channels,
        (),
    )
    merged, kept, _ = merge_stage(
        spot,
        ((out_kept, out_got), (reset_kept, reset_got), (value_kept, value_got)),
        (packed,),
    )
    got = dp_swap(merged, dp, 2)
    for bit in range(2, dp.bit_length() - 1):
        sent, kept, _ = line_stage(spot, kept, got, bit, ())
        got = dp_swap(sent, dp, 1 << bit)
    grad_out, grad_reset, grad_value = last_stage(
        spot, kept, got, model_width // dp, own_cols
    )
    head = packed.shape[1] - 2 * states
    small = jnp.sum(lax.all_to_all(packed, "tensor", 0, 0, tiled=True), axis=0)
    share = channels // dp
    everywhere = small[:head].reshape(2 * head, zdim)
    rates = jnp.pad(small.T, ((0, 0), (0, zdim - small.shape[0])))
    pieces = [
        jnp.broadcast_to(everywhere[None], (dp,) + everywhere.shape),
        g_shared.reshape(dp, share, zdim),
        rates.reshape(dp, share, zdim),
    ]
    small = jnp.sum(
        lax.all_to_all(jnp.concatenate(pieces, axis=1), "dp", 0, 0, tiled=True), axis=0
    )
    everywhere = small[: 2 * head]
    grad_shared = small[2 * head : 2 * head + share]
    rates = small[2 * head + share :]
    grad_forget = rates[:, head : head + states]
    grad_mix = rates[:, head + states : head + 2 * states]
    grad_skip = rates[:, 2 * model_width // channels + 2]
    gains = model_width // zdim
    return (
        block_output,
        grad_input,
        everywhere[:gains].reshape(model_width),
        grad_forget,
        grad_mix,
        grad_skip,
        grad_shared,
        everywhere[2 * gains],
        everywhere[2 * gains + 1],
        everywhere[2 * gains + 2],
        grad_value,
        grad_reset,
        grad_out,
        everywhere[gains : 2 * gains].reshape(model_width),
        grad_up,
        grad_down,
    )


def solution(mesh):
    in_specs = (
        P("dp", None, None),
        P("dp", None),
        P("dp", None),
        P(),
        P("tensor", None),
        P("tensor", None),
        P("tensor"),
        P(),
        P(),
        P(),
        P(),
        P(None, "tensor"),
        P(None, "tensor"),
        P("tensor", None),
        P(),
        P(None, "tensor"),
        P("tensor", None),
        P("dp", "tensor", None),
    )
    out_specs = (
        P("dp", "tensor", None),
        P("dp", "tensor", None),
        P(),
        P(("tensor", "dp"), None),
        P(("tensor", "dp"), None),
        P(("tensor", "dp")),
        P(("tensor", "dp"), None),
        P(),
        P(),
        P(),
        P("dp", "tensor"),
        P("dp", "tensor"),
        P(("tensor", "dp"), None),
        P(),
        P("dp", "tensor"),
        P(("tensor", "dp"), None),
    )
    return jax.shard_map(
        functools.partial(on_device, dp=mesh.shape["dp"]),
        mesh=mesh,
        in_specs=in_specs,
        out_specs=out_specs,
        check_vma=False,
    )
```
